512 devices in a mesh: section: 8 (over y_hi, x), expert: 16 (over z, core), dp: 4 (over y_lo).
Axes of the slice: x: 4, y: 8 (y_hi: 2, y_lo: 4; y = y_hi * 4 + y_lo), z: 8, core: 2. Of those that a mesh axis runs over, the one named last changes fastest.
Arguments:
- act: bfloat16 [8, 8192, 3584], P('section', ('expert', 'dp')), may hold values from -6 to 6
- cotangent: bfloat16 [8, 8192, 3584], P('section', ('expert', 'dp')), may hold values from -6 to 6
- expert_ids: int32 [8, 8192, 8], P('section', ('expert', 'dp')), may hold values from 0 to 255, as said below
- gate_values: float32 [8, 8192, 8], P('section', ('expert', 'dp')), may hold values from 0.05 to 0.5
- w_gate: bfloat16 [8, 3584, 2048], P('section', 'dp', 'expert'), may hold values from -0.09375 to 0.09375
- w_up: bfloat16 [8, 3584, 2048], P('section', 'dp', 'expert'), may hold values from -0.09375 to 0.09375
- w_down_t: bfloat16 [8, 3584, 2048], P('section', 'dp', 'expert'), may hold values from -0.1875 to 0.1875
Outputs:
- next_act: bfloat16 [8, 8192, 3584], P('section', ('expert', 'dp'))
- prev_grad: bfloat16 [8, 8192, 3584], P('section', ('expert', 'dp'))
- grad_gate: bfloat16 [8, 3584, 2048], P('section', 'dp', 'expert')
- grad_up: bfloat16 [8, 3584, 2048], P('section', 'dp', 'expert')
- grad_down_t: bfloat16 [8, 3584, 2048], P('section', 'dp', 'expert')
The draws below stay inside these ranges and needn't reach their ends.
Inputs may be any that keep to these rules, and one draw needn't show every extreme that they name: `expert_ids`: each row names 8 different experts. In each device's rows (aligned blocks of 128 rows) at most 16 rows name any one expert below 2; for each such expert some section and dp index have every block at exactly 16.
All inputs are finite; a program needn't handle non-finite values.
Results may differ from the reference program's by a relative error of at most 0.013.
Values may be sent and summed in bfloat16 or wider, within the bound.
A program may use at most 64 MiB of HBM per device.

```python
import math
import jax
import jax.numpy as jnp
from jax import lax

D = 3584
EXP_HIDDEN = 1024
NUM_EXP = 256
TOPK = 8
WIN_EXP = 2
CAP = 16
TOK_DEV = 128
SECTIONS = 8
TOKENS = 8192
COLS = 2048
HS = 128
N_EXPERT = 16
N_DP = 4


def route_table(key):
    blocks = SECTIONS * TOKENS // TOK_DEV
    per_section = TOKENS // TOK_DEV
    outside = NUM_EXP - WIN_EXP
    key_count, key_full, key_rank, key_other, key_order = jax.random.split(key, 5)
    counts = jax.random.randint(key_count, (blocks, WIN_EXP), 1, CAP + 1)
    key_section, key_replica = jax.random.split(key_full)
    full_section = jax.random.randint(key_section, (WIN_EXP,), 0, SECTIONS)
    full_replica = jax.random.randint(key_replica, (WIN_EXP,), 0, N_DP)
    block_ids = jnp.arange(blocks, dtype=jnp.int32)
    filled = (block_ids[:, None] // per_section == full_section[None, :]) & (block_ids[:, None] % N_DP == full_replica[None, :])
    counts = jnp.where(filled, CAP, counts)
    scores = jax.random.randint(key_rank, (blocks, WIN_EXP, TOK_DEV), 0, 1 << 18) * TOK_DEV + jnp.arange(TOK_DEV, dtype=jnp.int32)
    row_ranks = jnp.argsort(jnp.argsort(scores, axis=-1), axis=-1)
    picked = row_ranks < counts[:, :, None]
    picked = jnp.transpose(picked, (0, 2, 1)).reshape(blocks * TOK_DEV, WIN_EXP)
    other_scores = jax.random.randint(key_other, (blocks * TOK_DEV, outside), 0, 1 << 20) * outside + jnp.arange(outside, dtype=jnp.int32)
    top_values, chosen = lax.top_k(other_scores, TOPK)
    chosen = chosen.astype(jnp.int32) + WIN_EXP
    window_ids = jnp.where(picked, jnp.arange(WIN_EXP, dtype=jnp.int32)[None, :], chosen[:, :WIN_EXP])
    leading = jnp.concatenate([window_ids, chosen[:, WIN_EXP:]], axis=1)
    shuffle_keys = jax.random.randint(key_order, (blocks * TOK_DEV, TOPK), 0, 1 << 20) * TOPK + jnp.arange(TOPK, dtype=jnp.int32)
    column_order = jnp.argsort(shuffle_keys, axis=1)
    id_table = jnp.take_along_axis(leading, column_order, axis=1)
    return id_table.reshape(SECTIONS, TOKENS, TOPK).astype(jnp.int32)


def draw_expert_ids(key, part):
    key = jax.random.fold_in(key, 5)
    return route_table(key)


def shard_levels(stream_key, extent, shards, low, largest):
    def one(dim, shards_of):
        draws = jax.random.uniform(jax.random.fold_in(jax.random.fold_in(stream_key, 6), dim), (shards_of,), jnp.float32, low / len(shards), largest / len(shards))
        return jnp.repeat(jnp.exp(draws), extent[dim] // shards_of).reshape((-1,) + (1,) * (len(extent) - dim - 1))

    loudness = one(*shards[0])
    for cut in shards[1:]:
        loudness = loudness * one(*cut)
    return loudness


def bell_draw(own_key, dims, deviation, bound, pieces=(), held_as=jnp.bfloat16):
    values = jax.random.normal(own_key, dims, jnp.float32) * deviation
    if len(pieces) > 0:
        values = shard_levels(own_key, dims, pieces, -0.22, 0.18) * values
    return jnp.clip(values, min=-bound, max=bound).astype(held_as)


def setup_inputs(seed: int = 0) -> dict:
    splits = jax.random.split(jax.random.key(seed), 8)
    act = bell_draw(splits[0], (SECTIONS, TOKENS, D), 1.0, 6.0, ((0, 8), (1, 64)))
    cotangent = bell_draw(splits[1], (SECTIONS, TOKENS, D), 1.0, 6.0, ((0, 8), (1, 64)))
    expert_ids = draw_expert_ids(jax.random.fold_in(splits[7], 71), 0)
    gate_values = jnp.clip(jnp.exp(math.log(0.5) - 2.3025851 * jax.random.uniform(splits[3], (SECTIONS, TOKENS, TOPK), jnp.float32) ** shard_levels(splits[3], (SECTIONS, TOKENS, TOPK), ((0, 8), (1, 64)), -0.2, 0.2)), 0.05, 0.5)
    w_gate = bell_draw(splits[4], (SECTIONS, D, COLS), D ** -0.5, 0.09375, ((0, 8), (1, 4), (2, 16)))
    w_up = bell_draw(splits[5], (SECTIONS, D, COLS), D ** -0.5, 0.09375, ((0, 8), (1, 4), (2, 16)))
    w_down_t = bell_draw(splits[6], (SECTIONS, D, COLS), EXP_HIDDEN ** -0.5, 0.1875, ((0, 8), (1, 4), (2, 16)))
    return dict(act=act, cotangent=cotangent, expert_ids=expert_ids, gate_values=gate_values, w_gate=w_gate, w_up=w_up, w_down_t=w_down_t)


def rounded(values):
    return lax.optimization_barrier(values.astype(jnp.bfloat16)).astype(jnp.float32)

def section_pass(act_rows, cot_rows, id_rows, gate_rows, gate_section, up_section, down_section):
    blocks = TOKENS // TOK_DEV
    group_size = N_EXPERT // WIN_EXP
    buffer_rows = blocks * CAP
    x_float = act_rows.astype(jnp.float32)
    inv_root = lax.rsqrt(lax.optimization_barrier(jnp.mean(x_float * x_float, axis=-1, keepdims=True)) + 1e-06)
    normed = x_float * inv_root
    rows_in = normed.astype(jnp.bfloat16)
    cot_float = cot_rows.astype(jnp.float32)
    combined = jnp.zeros_like(x_float)
    normed_grad = jnp.zeros_like(x_float)
    block_start = jnp.arange(TOKENS, dtype=jnp.int32) // TOK_DEV * CAP
    grad_list = []
    for expert in range(WIN_EXP):
        named_rows = id_rows == expert
        gate_of = lax.optimization_barrier(jnp.sum(jnp.where(named_rows, gate_rows, 0.0), axis=-1))
        routed = jnp.any(named_rows, axis=-1)
        within = jnp.cumsum(routed.reshape(blocks, TOK_DEV).astype(jnp.int32), axis=1).reshape(TOKENS) - 1
        target = jnp.where(routed, block_start + within, buffer_rows).astype(jnp.int32)
        grad_rows = (gate_of[:, None] * cot_float).astype(jnp.bfloat16)
        expert_in = jnp.zeros((buffer_rows + 1, D), jnp.bfloat16).at[target].set(rows_in)[:-1]
        expert_grad = jnp.zeros((buffer_rows + 1, D), jnp.bfloat16).at[target].set(grad_rows)[:-1]
        gate_cols = gate_section[:, expert * EXP_HIDDEN:(expert + 1) * EXP_HIDDEN]
        up_cols = up_section[:, expert * EXP_HIDDEN:(expert + 1) * EXP_HIDDEN]
        down_cols = down_section[:, expert * EXP_HIDDEN:(expert + 1) * EXP_HIDDEN]
        pre_gate = jnp.dot(expert_in, gate_cols, preferred_element_type=jnp.float32)
        pre_up = jnp.dot(expert_in, up_cols, preferred_element_type=jnp.float32)
        hidden_grad = jnp.dot(expert_grad, down_cols, preferred_element_type=jnp.float32)
        sig = jax.nn.sigmoid(pre_gate)
        silu_gate = pre_gate * sig
        hidden_act = (silu_gate * pre_up).astype(jnp.bfloat16)
        d_gate = (hidden_grad * pre_up * sig * (1.0 + pre_gate * (1.0 - sig))).astype(jnp.bfloat16)
        d_up = (hidden_grad * silu_gate).astype(jnp.bfloat16)
        hidden_parts = hidden_act.astype(jnp.float32).reshape(buffer_rows, group_size, HS)
        gate_parts = d_gate.astype(jnp.float32).reshape(buffer_rows, group_size, HS)
        up_parts = d_up.astype(jnp.float32).reshape(buffer_rows, group_size, HS)
        gate_slices = gate_cols.astype(jnp.float32).reshape(D, group_size, HS)
        up_slices = up_cols.astype(jnp.float32).reshape(D, group_size, HS)
        down_slices = down_cols.astype(jnp.float32).reshape(D, group_size, HS)
        out_parts = jnp.einsum('rgh,dgh->grd', hidden_parts, down_slices, precision=lax.Precision.HIGHEST)
        expert_out = lax.optimization_barrier(jnp.sum(rounded(out_parts), axis=0))
        back_parts = jnp.einsum('rgh,dgh->grd', gate_parts, gate_slices, precision=lax.Precision.HIGHEST)
        back_parts = back_parts + jnp.einsum('rgh,dgh->grd', up_parts, up_slices, precision=lax.Precision.HIGHEST)
        input_grad = lax.optimization_barrier(jnp.sum(rounded(back_parts), axis=0))
        in_rep = expert_in.astype(jnp.float32).reshape(N_EXPERT, N_DP, CAP, D)
        grad_rep = expert_grad.astype(jnp.float32).reshape(N_EXPERT, N_DP, CAP, D)
        dg_rep = gate_parts.reshape(N_EXPERT, N_DP, CAP, EXP_HIDDEN)
        du_rep = up_parts.reshape(N_EXPERT, N_DP, CAP, EXP_HIDDEN)
        act_rep = hidden_parts.reshape(N_EXPERT, N_DP, CAP, EXP_HIDDEN)
        part_gate = jnp.einsum('jdcf,jdch->dfh', in_rep, dg_rep, precision=lax.Precision.HIGHEST)
        part_up = jnp.einsum('jdcf,jdch->dfh', in_rep, du_rep, precision=lax.Precision.HIGHEST)
        part_down = jnp.einsum('jdcf,jdch->dfh', grad_rep, act_rep, precision=lax.Precision.HIGHEST)
        grad_list.append((lax.optimization_barrier(jnp.sum(rounded(part_gate), axis=0)).astype(jnp.bfloat16), lax.optimization_barrier(jnp.sum(rounded(part_up), axis=0)).astype(jnp.bfloat16), lax.optimization_barrier(jnp.sum(rounded(part_down), axis=0)).astype(jnp.bfloat16)))
        picked = jnp.minimum(target, buffer_rows - 1)
        combined = combined + gate_of[:, None] * jnp.where(routed[:, None], jnp.take(expert_out, picked, axis=0), 0.0)
        normed_grad = normed_grad + jnp.where(routed[:, None], jnp.take(input_grad, picked, axis=0), 0.0)
    section_out = (x_float + combined).astype(jnp.bfloat16)
    spread = lax.optimization_barrier(jnp.mean(normed * normed_grad, axis=-1, keepdims=True))
    row_grad = (cot_float + inv_root * (normed_grad - normed * spread)).astype(jnp.bfloat16)
    grad_gate = jnp.concatenate([item[0] for item in grad_list], axis=1)
    grad_up = jnp.concatenate([item[1] for item in grad_list], axis=1)
    grad_down = jnp.concatenate([item[2] for item in grad_list], axis=1)
    return (section_out, row_grad, grad_gate, grad_up, grad_down)

def reference(act, cotangent, expert_ids, gate_values, w_gate, w_up, w_down_t):
    outs_list, grads_list, gate_list, up_list, down_list = ([], [], [], [], [])
    for section in range(SECTIONS):
        result = section_pass(act[section], cotangent[section], expert_ids[section], gate_values[section], w_gate[section], w_up[section], w_down_t[section])
        outs_list.append(result[0])
        grads_list.append(result[1])
        gate_list.append(result[2])
        up_list.append(result[3])
        down_list.append(result[4])
    next_act = jnp.roll(jnp.stack(outs_list), 1, axis=0)
    prev_grad = jnp.roll(jnp.stack(grads_list), -1, axis=0)
    return (next_act, prev_grad, jnp.stack(gate_list), jnp.stack(up_list), jnp.stack(down_list))
```

```python
import functools

import jax
import jax.numpy as jnp
from jax import lax
from jax.experimental import pallas as pl
from jax.experimental.pallas import tpu as pltpu
from jax.sharding import PartitionSpec as P

MESH = pl.DeviceIdType.MESH
EXPERTS = 2
CAP = 16
F32 = jnp.float32
BF16 = jnp.bfloat16


def dot(left, right, left_dim, right_dim, precision=None):
    return lax.dot_general(
        left,
        right,
        (((left_dim,), (right_dim,)), ((), ())),
        preferred_element_type=F32,
        precision=precision,
    )


def kernel(
    act, cot, ids, gates, w_gate, w_up, w_down,
    next_act, prev_grad, d_gate_out, d_up_out, d_down_out,
    wf, pk, rb, xg, picks, pick_prev, pick_next, act_in, cot_in,
    normed, hp, hf, hr, ag, yp, rs, ef, fin, ysend, dsend, yin, din, dw_mine, dw_send, dw_in,
    w_s, w_r, a_s, a_r, sh_s, sh_r, bi_s, bo_s, b_r, p_s, p_r, g_s, g_r,
    di_s, do_s, d_r, e_s, e_r, x_s, x_r, q_s, q_r,
):
    sec, ex, d = lax.axis_index("section"), lax.axis_index("expert"), lax.axis_index("dp")
    z, c = ex // 2, ex % 2
    q, half = z % 4, z // 4
    sgn = 1 - 2 * (q // 2)
    qm = q * (1 - q // 2) + (3 - q) * (q // 2)
    edge = 1 - qm
    is_edge, is_inner = qm == 0, qm == 1
    width = act.shape[1]
    chunk = width // 4
    cols = w_gate.shape[1]

    def z_dev(step):
        return {"expert": lax.rem(z + step + 8, 8) * 2 + c}

    inward, outward = z_dev(sgn), z_dev(-sgn)
    sibling = {"expert": z * 2 + 1 - c}
    dp_dev = [{"dp": lax.rem(d + r + 1, 4)} for r in range(3)]
    sec_next = {"section": lax.rem(sec + 1, 8)}
    sec_prev = {"section": lax.rem(sec + 7, 8)}

    bar = pltpu.get_barrier_semaphore()
    for dev in (inward, outward, sibling, *dp_dev, sec_next, sec_prev):
        pl.semaphore_signal(bar, inc=1, device_id=dev, device_id_type=MESH)
    pl.semaphore_wait(bar, 8)

    pending = []

    def make(src, dst, s, r, dev):
        return pltpu.make_async_remote_copy(
            src_ref=src, dst_ref=dst, send_sem=s, recv_sem=r, device_id=dev, device_id_type=MESH
        )

    def send(src, dst, s, r, dev, pred=None):
        def build():
            return make(src, dst, s, r, dev)

        if pred is None:
            build().start()
        else:
            pl.when(pred)(lambda: build().start())
        pending.append((pred, build))

    def arrived(dst, r, s, dev):
        make(dst, dst, s, r, dev).wait_recv()

    base = [0, 1, -1, 2, -2, 3, -3 + 7 * edge, 4 + edge]
    group = [lax.rem(z + sgn * b + 16, 8) for b in base]

    mine = pl.ds(pl.multiple_of(c * cols, cols), cols)
    for k, w in enumerate((w_gate, w_up, w_down)):
        at = pl.ds(pl.multiple_of(2 * cols * k + c * cols, cols), cols)
        send(w, wf.at[:, at], w_s.at[k], w_r.at[k], sibling)
        wf[:, at] = w[...]

    tokens = act.shape[0]
    upper = (
        lax.broadcasted_iota(jnp.int32, (tokens, tokens), 0)
        <= lax.broadcasted_iota(jnp.int32, (tokens, tokens), 1)
    ).astype(BF16)
    slots = lax.broadcasted_iota(jnp.int32, (CAP, tokens), 0).astype(F32)
    ones = jnp.ones((8, ids.shape[1]), F32)
    slot_gate = []
    for e in range(EXPERTS):
        named = ids[...] == e
        gate_of = dot(ones, jnp.where(named, gates[...], 0.0), 1, 1, lax.Precision.HIGHEST)[0:1]
        routed = dot(ones, jnp.where(named, 1.0, 0.0), 1, 1)
        within = dot(routed.astype(BF16), upper, 1, 0)[0:1] - 1.0
        pick = jnp.where((slots == within) & (routed[0:1] > 0.5), 1.0, 0.0)
        slot_gate.append(jnp.sum(pick * gate_of, axis=1, keepdims=True))
        picks[e * CAP : (e + 1) * CAP] = pick.astype(BF16)
    slot_gates = jnp.concatenate(slot_gate, axis=0)
    x_rows = dot(picks[...], act[...], 1, 0)
    inv_root = lax.rsqrt(jnp.mean(x_rows * x_rows, axis=1, keepdims=True) + 1e-6)
    x_rows = x_rows * inv_root
    normed[...] = x_rows
    x_rows = x_rows.astype(BF16)
    g_rows = (slot_gates * dot(picks[...], cot[...], 1, 0)).astype(BF16)
    for e in range(EXPERTS):
        pk[e, 0] = x_rows[e * CAP : (e + 1) * CAP]
        pk[e, 1] = g_rows[e * CAP : (e + 1) * CAP]

    for r in range(3):
        there = lax.rem(d + r + 1, 4)
        at = pl.ds(pl.multiple_of(there * chunk, 128), chunk)
        send(pk.at[:, :, :, at], rb.at[:, :, d], a_s.at[r], a_r.at[r], dp_dev[r])
    own_at = pl.ds(pl.multiple_of(d * chunk, 128), chunk)
    for e in range(EXPERTS):
        for t in range(2):
            rb[e, t, d] = pk[e, t, :, own_at]
    for r in range(3):
        arrived(rb.at[:, :, lax.rem(d + 3 - r, 4)], a_r.at[r], a_s.at[r], dp_dev[r])

    send(rb.at[1 - half], xg.at[8 + (z - 8) * edge], bo_s.at[8], b_r.at[8 + (z - 8) * edge], outward)
    send(rb.at[half], xg.at[z], bi_s.at[0], b_r.at[z], inward)
    send(rb.at[half], xg.at[z], bo_s.at[0], b_r.at[z], outward, is_inner)

    send(picks, pick_prev, sh_s.at[2], sh_r.at[2], sec_next)
    send(picks, pick_next, sh_s.at[3], sh_r.at[3], sec_prev)
    send(act, act_in, sh_s.at[0], sh_r.at[0], sec_next)
    send(cot, cot_in, sh_s.at[1], sh_r.at[1], sec_prev)

    xg[z] = rb[half]
    for k in range(3):
        at = pl.ds(pl.multiple_of(2 * cols * k + (1 - c) * cols, cols), cols)
        arrived(wf.at[:, at], w_r.at[k], w_s.at[k], sibling)

    hidden = 2 * cols
    rows = 4 * CAP

    def front(j):
        g = group[j]
        if j == 1:
            inner = lax.rem(z + sgn + 8, 8)

            @pl.when(is_edge)
            def _():
                arrived(xg.at[8], b_r.at[8], bo_s.at[9], inward)

            send(xg.at[8], xg.at[inner], bo_s.at[9], b_r.at[inner], outward, is_edge)
        if j > 0:
            arrived(xg.at[g], b_r.at[g], bo_s.at[0], inward)
        if j in (1, 3, 5, 7):
            send(xg.at[g], xg.at[g], bo_s.at[j], b_r.at[g], outward, is_inner)
        elif j in (2, 4):
            send(xg.at[g], xg.at[g], bi_s.at[j], b_r.at[g], inward)
        elif j == 6:
            send(xg.at[g], xg.at[g], bi_s.at[j], b_r.at[g], inward, is_inner)
        x = xg[g, 0].reshape(rows, chunk)
        gr = xg[g, 1].reshape(rows, chunk)
        part = jnp.concatenate(
            [dot(x, wf[:, : 2 * hidden], 1, 0), dot(gr, wf[:, 2 * hidden :], 1, 0)], axis=1
        ).reshape(4, CAP, 3 * hidden)
        hf[j] = part
        hp[j] = part.astype(BF16)
        for r in range(3):
            there = lax.rem(d + r + 1, 4)
            send(hp.at[j, there], hr.at[j, r], p_s.at[j, r], p_r.at[j, r], dp_dev[r])

    def middle(j):
        g = group[j]
        total = hf[j, d]
        for r in range(3):
            arrived(hr.at[j, r], p_r.at[j, r], p_s.at[j, r], dp_dev[r])
            total = total + hr[j, r].astype(F32)
        pre_gate = total[:, :hidden]
        pre_up = total[:, hidden : 2 * hidden]
        hidden_grad = total[:, 2 * hidden :]
        sig = jax.nn.sigmoid(pre_gate)
        silu = pre_gate * sig
        ag[g, d, :, :hidden] = (hidden_grad * pre_up * sig * (1.0 + pre_gate * (1.0 - sig))).astype(BF16)
        ag[g, d, :, hidden : 2 * hidden] = (hidden_grad * silu).astype(BF16)
        ag[g, d, :, 2 * hidden :] = (silu * pre_up).astype(BF16)
        for r in range(3):
            send(ag.at[g, d], ag.at[g, d], g_s.at[j, r], g_r.at[j, r], dp_dev[r])

    def back(j):
        g = group[j]
        for r in range(3):
            arrived(ag.at[g, lax.rem(d + 3 - r, 4)], g_r.at[j, r], g_s.at[j, r], dp_dev[r])
        h = ag[g].reshape(rows, 3 * hidden)
        y = dot(h[:, 2 * hidden :], wf[:, 2 * hidden :], 1, 1)
        dx = dot(h[:, : 2 * hidden], wf[:, : 2 * hidden], 1, 1)
        yp[g, 0] = y.astype(BF16).reshape(4, CAP, chunk)
        yp[g, 1] = dx.astype(BF16).reshape(4, CAP, chunk)
        if j in (1, 3, 5, 6, 7):
            slot = 8 if j == 1 else g
            send(yp.at[g], rs.at[slot], di_s.at[j], d_r.at[slot], inward, is_edge)

    for j in range(8):
        front(j)
        if j >= 1:
            middle(j - 1)
        if j >= 2:
            back(j - 2)
    middle(7)
    back(6)
    back(7)

    def add(g, slot):
        yp[g] = (yp[g].astype(F32) + rs[slot].astype(F32)).astype(BF16)

    def chain(j):
        g = group[j]
        arrived(rs.at[g], d_r.at[g], do_s.at[0], inward)
        add(g, g)

    for j in (1, 3, 2, 5, 4, 7, 6):
        g = group[j]
        if j in (2, 4):
            chain(j)
            send(yp.at[g], rs.at[g], do_s.at[j], d_r.at[g], outward, is_inner)
            slot = 9 if j == 2 else 10
            send(yp.at[g], rs.at[slot], do_s.at[j], d_r.at[slot], outward, is_edge)
        else:
            pl.when(is_inner)(functools.partial(chain, j))
            if j == 6:
                send(yp.at[g], rs.at[g], do_s.at[j], d_r.at[g], outward, is_inner)
            else:
                send(yp.at[g], rs.at[g], di_s.at[j], d_r.at[g], inward, is_inner)

    @pl.when(is_edge)
    def _():
        arrived(rs.at[10], d_r.at[10], do_s.at[0], outward)

    send(rs.at[10], rs.at[9], di_s.at[2], d_r.at[9], inward, is_edge)

    arrived(rs.at[z], d_r.at[z], do_s.at[0], inward)
    add(z, z)

    @pl.when(is_inner)
    def _():
        arrived(rs.at[8], d_r.at[8], do_s.at[0], outward)
        add(z, 8)

    def home(src, e, k):
        for r in range(3):
            there = lax.rem(d + r + 1, 4)
            send(src.at[:, there], fin.at[e, :, :, own_at], e_s.at[k, r], e_r.at[k, r], dp_dev[r])
        fin[e, :, :, own_at] = src[:, d]

    home(yp.at[z], half, 0)
    arrived(rs.at[9], d_r.at[9], do_s.at[0], outward)
    home(rs.at[9], 1 - half, 1)

    h_all = ag[...].reshape(8 * rows, 3 * hidden)
    x_all = xg[0:8, 0].reshape(8 * rows, chunk)
    dw_mine[:, : 2 * hidden] = dot(x_all, h_all[:, : 2 * hidden], 0, 0)
    g_all = xg[0:8, 1].reshape(8 * rows, chunk)
    dw_mine[:, 2 * hidden :] = dot(g_all, h_all[:, 2 * hidden :], 0, 0)
    for k in range(3):
        at = pl.ds(pl.multiple_of(hidden * k + (1 - c) * cols, cols), cols)
        dw_send[k] = dw_mine[:, at].astype(BF16)
        send(dw_send.at[k], dw_in.at[k], q_s.at[k], q_r.at[k], sibling)

    for k, e in ((0, half), (1, 1 - half)):
        for r in range(3):
            there = lax.rem(d + 3 - r, 4)
            at = pl.ds(pl.multiple_of(there * chunk, 128), chunk)
            arrived(fin.at[e, :, :, at], e_r.at[k, r], e_s.at[k, r], dp_dev[r])
    y_rows = fin[:, 0].reshape(EXPERTS * CAP, width).astype(F32)
    ysend[...] = (slot_gates * y_rows).astype(BF16)
    send(ysend, yin, x_s.at[0], x_r.at[0], sec_next)
    d_rows = fin[:, 1].reshape(EXPERTS * CAP, width).astype(F32)
    spread = jnp.mean(normed[...] * d_rows, axis=1, keepdims=True)
    dsend[...] = (inv_root * (d_rows - normed[...] * spread)).astype(BF16)
    send(dsend, din, x_s.at[1], x_r.at[1], sec_prev)

    for k, out in enumerate((d_gate_out, d_up_out, d_down_out)):
        arrived(dw_in.at[k], q_r.at[k], q_s.at[k], sibling)
        at = pl.ds(pl.multiple_of(hidden * k + c * cols, cols), cols)
        out[...] = (dw_mine[:, at] + dw_in[k].astype(F32)).astype(BF16)

    arrived(pick_prev, sh_r.at[2], sh_s.at[2], sec_next)
    arrived(act_in, sh_r.at[0], sh_s.at[0], sec_next)
    arrived(yin, x_r.at[0], x_s.at[0], sec_next)
    next_act[...] = (act_in[...].astype(F32) + dot(pick_prev[...], yin[...], 0, 0)).astype(BF16)
    arrived(pick_next, sh_r.at[3], sh_s.at[3], sec_prev)
    arrived(cot_in, sh_r.at[1], sh_s.at[1], sec_prev)
    arrived(din, x_r.at[1], x_s.at[1], sec_prev)
    prev_grad[...] = (cot_in[...].astype(F32) + dot(pick_next[...], din[...], 0, 0)).astype(BF16)

    for pred, build in pending:
        if pred is None:
            build().wait_send()
        else:
            pl.when(pred)(lambda build=build: build().wait_send())


def per_device(act, cotangent, expert_ids, gate_values, w_gate, w_up, w_down_t):
    tokens, width = act.shape[1:]
    depth, cols = w_gate.shape[1:]
    chunk, hidden = width // 4, 2 * cols
    vmem = pl.BlockSpec(memory_space=pltpu.VMEM)
    dma = pltpu.SemaphoreType.DMA
    slots = EXPERTS * CAP
    outs = pl.pallas_call(
        kernel,
        name="moe_relay",
        out_shape=[
            jax.ShapeDtypeStruct((tokens, width), BF16),
            jax.ShapeDtypeStruct((tokens, width), BF16),
            jax.ShapeDtypeStruct((depth, cols), BF16),
            jax.ShapeDtypeStruct((depth, cols), BF16),
            jax.ShapeDtypeStruct((depth, cols), BF16),
        ],
        in_specs=[vmem] * 7,
        out_specs=[vmem] * 5,
        scratch_shapes=[
            pltpu.VMEM((depth, 3 * hidden), BF16),
            pltpu.VMEM((EXPERTS, 2, CAP, width), BF16),
            pltpu.VMEM((EXPERTS, 2, 4, CAP, chunk), BF16),
            pltpu.VMEM((9, 2, 4, CAP, chunk), BF16),
            pltpu.VMEM((slots, tokens), BF16),
            pltpu.VMEM((slots, tokens), BF16),
            pltpu.VMEM((slots, tokens), BF16),
            pltpu.VMEM((tokens, width), BF16),
            pltpu.VMEM((tokens, width), BF16),
            pltpu.VMEM((slots, width), F32),
            pltpu.VMEM((8, 4, CAP, 3 * hidden), BF16),
            pltpu.VMEM((8, 4, CAP, 3 * hidden), F32),
            pltpu.VMEM((8, 3, CAP, 3 * hidden), BF16),
            pltpu.VMEM((8, 4, CAP, 3 * hidden), BF16),
            pltpu.VMEM((8, 2, 4, CAP, chunk), BF16),
            pltpu.VMEM((11, 2, 4, CAP, chunk), BF16),
            pltpu.VMEM((2, 4, CAP, chunk), BF16),
            pltpu.VMEM((EXPERTS, 2, CAP, width), BF16),
            pltpu.VMEM((slots, width), BF16),
            pltpu.VMEM((slots, width), BF16),
            pltpu.VMEM((slots, width), BF16),
            pltpu.VMEM((slots, width), BF16),
            pltpu.VMEM((depth, 3 * hidden), F32),
            pltpu.VMEM((3, depth, cols), BF16),
            pltpu.VMEM((3, depth, cols), BF16),
            dma((3,)), dma((3,)),
            dma((3,)), dma((3,)),
            dma((4,)), dma((4,)),
            dma((8,)), dma((10,)), dma((9,)),
            dma((8, 3)), dma((8, 3)),
            dma((8, 3)), dma((8, 3)),
            dma((8,)), dma((8,)), dma((11,)),
            dma((2, 3)), dma((2, 3)),
            dma((2,)), dma((2,)),
            dma((3,)), dma((3,)),
        ],
        compiler_params=pltpu.CompilerParams(
            collective_id=0, has_side_effects=True, vmem_limit_bytes=50 * 2**20
        ),
    )(act[0], cotangent[0], expert_ids[0], gate_values[0], w_gate[0], w_up[0], w_down_t[0])
    return tuple(out[None] for out in outs)


def solution(mesh):
    rows = P("section", ("expert", "dp"), None)
    weights = P("section", "dp", "expert")
    return jax.shard_map(
        per_device,
        mesh=mesh,
        in_specs=(rows,) * 4 + (weights,) * 3,
        out_specs=(rows,) * 2 + (weights,) * 3,
        check_vma=False,
    )
```

```python
import jax
import jax.numpy as jnp
from jax import lax
from jax.experimental import pallas as pl
from jax.experimental.pallas import tpu as pltpu
from jax.sharding import PartitionSpec as P

MESH = pl.DeviceIdType.MESH
EXPERTS = 2
CAP = 16
F32 = jnp.float32
BF16 = jnp.bfloat16


def dot(left, right, left_dim, right_dim, precision=None):
    return lax.dot_general(
        left,
        right,
        (((left_dim,), (right_dim,)), ((), ())),
        preferred_element_type=F32,
        precision=precision,
    )


def kernel(
    act_h, cot_h, ids_h, gates_h, w_gate, w_up, w_down,
    next_act, prev_grad, d_gate_out, d_up_out, d_down_out,
    act, cot, ids, gates,
    wf, pk, rb, xg, picks, pick_prev, pick_next, act_in, cot_in, via_in, via_out,
    normed, hp, hf, hr, ag, yp, rs, fin, ysend, dsend, yin, din, dw_mine, dw_send, dw_in,
    l_s, w_s, w_r, a_s, a_r, sh_s, sh_r, bi_s, bo_s, b_r, p_s, p_r, g_s, g_r,
    di_s, do_s, d_r, e_s, e_r, x_s, x_r, q_s, q_r,
):
    sec, ex, d = lax.axis_index("section"), lax.axis_index("expert"), lax.axis_index("dp")
    z, c = ex // 2, ex % 2
    q, half = z % 4, z // 4
    sx, sy = sec % 4, sec // 4
    sgn = 1 - 2 * (q // 2)
    qm = q * (1 - q // 2) + (3 - q) * (q // 2)
    edge = 1 - qm
    is_edge, is_inner = qm == 0, qm == 1
    width = act.shape[1]
    chunk = width // 4
    cols = w_gate.shape[1]

    def z_dev(step):
        return {"expert": lax.rem(z + step + 8, 8) * 2 + c}

    inward, outward, beyond = z_dev(sgn), z_dev(-sgn), z_dev(-2 * sgn)
    sibling = {"expert": z * 2 + 1 - c}
    dp_dev = [{"dp": lax.rem(d + r + 1, 4)} for r in range(3)]
    sec_next = {"section": lax.rem(sec + 1, 8)}
    sec_prev = {"section": lax.rem(sec + 7, 8)}
    sec_skip = {"section": sy * 4 + lax.rem(sx + 2, 4)}
    sec_over = {"section": lax.rem(sec + 4, 8)}

    def fetch(src, dst, k):
        copy = pltpu.make_async_copy(src, dst, l_s.at[k])
        copy.start()
        return copy

    small = [fetch(ids_h, ids, 0), fetch(gates_h, gates, 1)]
    big = [fetch(act_h, act, 2), fetch(cot_h, cot, 3)]
    weights = []
    for k, w in enumerate((w_gate, w_up, w_down)):
        at = pl.ds(pl.multiple_of(2 * cols * k + c * cols, cols), cols)
        weights.append(fetch(w, wf.at[:, at], 4 + k))

    bar = pltpu.get_barrier_semaphore()
    partners = (inward, outward, beyond, sibling, *dp_dev, sec_next, sec_prev, sec_skip, sec_over)
    for dev in partners:
        pl.semaphore_signal(bar, inc=1, device_id=dev, device_id_type=MESH)

    for copy in small:
        copy.wait()
    tokens = act.shape[0]
    upper = (
        lax.broadcasted_iota(jnp.int32, (tokens, tokens), 0)
        <= lax.broadcasted_iota(jnp.int32, (tokens, tokens), 1)
    ).astype(BF16)
    slots = lax.broadcasted_iota(jnp.int32, (CAP, tokens), 0).astype(F32)
    slot_gate = []
    for e in range(EXPERTS):
        named = jnp.where(ids[...] == e, 1.0, 0.0)
        gate_of = jnp.sum(named * gates[...], axis=0, keepdims=True)
        routed = jnp.sum(named, axis=0, keepdims=True)
        within = dot(jnp.broadcast_to(routed, (8, tokens)).astype(BF16), upper, 1, 0)[0:1] - 1.0
        pick = jnp.where((slots == within) & (routed > 0.5), 1.0, 0.0)
        slot_gate.append(jnp.sum(pick * gate_of, axis=1, keepdims=True))
        picks[e * CAP : (e + 1) * CAP] = pick.astype(BF16)
    slot_gates = jnp.concatenate(slot_gate, axis=0)
    for copy in big:
        copy.wait()
    x_rows = dot(picks[...], act[...], 1, 0)
    inv_root = lax.rsqrt(jnp.mean(x_rows * x_rows, axis=1, keepdims=True) + 1e-6)
    x_rows = x_rows * inv_root
    normed[...] = x_rows
    x_rows = x_rows.astype(BF16)
    g_rows = (slot_gates * dot(picks[...], cot[...], 1, 0)).astype(BF16)
    for e in range(EXPERTS):
        pk[e, 0] = x_rows[e * CAP : (e + 1) * CAP]
        pk[e, 1] = g_rows[e * CAP : (e + 1) * CAP]
    for copy in weights:
        copy.wait()

    pl.semaphore_wait(bar, len(partners))

    pending = []

    def make(src, dst, s, r, dev):
        return pltpu.make_async_remote_copy(
            src_ref=src, dst_ref=dst, send_sem=s, recv_sem=r, device_id=dev, device_id_type=MESH
        )

    def send(src, dst, s, r, dev, pred=None):
        def build():
            return make(src, dst, s, r, dev)

        if pred is None:
            build().start()
        else:
            pl.when(pred)(lambda: build().start())
        pending.append((pred, build))

    def arrived(dst, r, s, dev):
        make(dst, dst, s, r, dev).wait_recv()

    at_edge, at_inner = (0, -2, -1, 1, 2, 3, 5, 4), (0, 1, -1, 2, -3, -2, 4, 3)
    group = [lax.rem(z + sgn * (i + edge * (o - i)) + 16, 8) for o, i in zip(at_edge, at_inner)]

    for r in range(3):
        there = lax.rem(d + r + 1, 4)
        at = pl.ds(pl.multiple_of(there * chunk, 128), chunk)
        send(pk.at[:, :, :, at], rb.at[:, :, d], a_s.at[r], a_r.at[r], dp_dev[r])
    own_at = pl.ds(pl.multiple_of(d * chunk, 128), chunk)
    for e in range(EXPERTS):
        for t in range(2):
            rb[e, t, d] = pk[e, t, :, own_at]
    for k, w in enumerate((w_gate, w_up, w_down)):
        at = pl.ds(pl.multiple_of(2 * cols * k + c * cols, cols), cols)
        send(w, wf.at[:, at], w_s.at[k], w_r.at[k], sibling)
    for r in range(3):
        arrived(rb.at[:, :, lax.rem(d + 3 - r, 4)], a_r.at[r], a_s.at[r], dp_dev[r])

    reach = z_dev(-sgn * (1 + qm))
    for t in range(2):
        send(rb.at[1 - half, t], xg.at[z, t], bo_s.at[8, t], b_r.at[z, t], reach)
        send(rb.at[half, t], xg.at[z, t], bi_s.at[0, t], b_r.at[z, t], inward)
    for t in range(2):
        send(rb.at[half, t], xg.at[z, t], bo_s.at[0, t], b_r.at[z, t], outward, is_inner)

    mid = tokens // 2
    low, high = pl.ds(0, mid), pl.ds(mid, mid)
    send(picks, pick_prev, sh_s.at[4], sh_r.at[4], sec_next)
    send(picks, pick_next, sh_s.at[5], sh_r.at[5], sec_prev)
    send(act.at[high], via_in, sh_s.at[1], sh_r.at[6], sec_skip, sx == 3)
    send(cot.at[high], via_in, sh_s.at[3], sh_r.at[6], sec_skip, sx == 0)
    for k, rows in ((0, low), (1, high)):
        send(act.at[rows], act_in.at[rows], sh_s.at[k], sh_r.at[k], sec_next, sx != 3)
        send(cot.at[rows], cot_in.at[rows], sh_s.at[2 + k], sh_r.at[2 + k], sec_prev, sx != 0)
    is_via = (sx == 1) | (sx == 2)

    xg[z] = rb[half]
    for k in range(3):
        at = pl.ds(pl.multiple_of(2 * cols * k + (1 - c) * cols, cols), cols)
        arrived(wf.at[:, at], w_r.at[k], w_s.at[k], sibling)

    hidden = 2 * cols
    rows = 4 * CAP

    def front(j):
        g = group[j]
        for t in range(2):
            if j > 0:
                arrived(xg.at[g, t], b_r.at[g, t], bo_s.at[0, t], inward)
            if j in (1, 2):
                send(xg.at[g, t], xg.at[g, t], bi_s.at[j, t], b_r.at[g, t], inward, is_edge)
            if j in (1, 3, 6, 7):
                send(xg.at[g, t], xg.at[g, t], bo_s.at[j, t], b_r.at[g, t], outward, is_inner)
            if j in (2, 4, 5):
                send(xg.at[g, t], xg.at[g, t], bi_s.at[j, t], b_r.at[g, t], inward, is_inner)
        x = xg[g, 0].reshape(rows, chunk)
        gr = xg[g, 1].reshape(rows, chunk)
        part = jnp.concatenate(
            [dot(x, wf[:, : 2 * hidden], 1, 0), dot(gr, wf[:, 2 * hidden :], 1, 0)], axis=1
        ).reshape(4, CAP, 3 * hidden)
        hf[j] = part
        hp[j] = part.astype(BF16)
        for r in range(3):
            there = lax.rem(d + r + 1, 4)
            send(hp.at[j, there], hr.at[j, r], p_s.at[j, r], p_r.at[j, r], dp_dev[r])

    def middle(j):
        g = group[j]
        total = hf[j, d]
        for r in range(3):
            arrived(hr.at[j, r], p_r.at[j, r], p_s.at[j, r], dp_dev[r])
            total = total + hr[j, r].astype(F32)
        pre_gate = total[:, :hidden]
        pre_up = total[:, hidden : 2 * hidden]
        hidden_grad = total[:, 2 * hidden :]
        sig = jax.nn.sigmoid(pre_gate)
        silu = pre_gate * sig
        ag[g, d, :, :hidden] = (hidden_grad * pre_up * sig * (1.0 + pre_gate * (1.0 - sig))).astype(BF16)
        ag[g, d, :, hidden : 2 * hidden] = (hidden_grad * silu).astype(BF16)
        ag[g, d, :, 2 * hidden :] = (silu * pre_up).astype(BF16)
        for r in range(3):
            send(ag.at[g, d], ag.at[g, d], g_s.at[j, r], g_r.at[j, r], dp_dev[r])

    def back(j):
        g = group[j]
        for r in range(3):
            arrived(ag.at[g, lax.rem(d + 3 - r, 4)], g_r.at[j, r], g_s.at[j, r], dp_dev[r])
        h = ag[g].reshape(rows, 3 * hidden)
        slot = 8 if j == 3 else g
        for t, (a, b) in enumerate(((2 * hidden, 3 * hidden), (0, 2 * hidden))):
            yp[g, t] = dot(h[:, a:b], wf[:, a:b], 1, 1).astype(BF16).reshape(4, CAP, chunk)
            if j >= 3:
                send(yp.at[g, t], rs.at[slot, t], di_s.at[j, t], d_r.at[slot, t], inward, is_edge)

    def add(g, t, slot):
        yp[g, t] = (yp[g, t].astype(F32) + rs[slot, t].astype(F32)).astype(BF16)

    def chain(j, pred, s, dev, slot=None):
        g = group[j]
        slot = g if slot is None else slot
        for t in range(2):

            @pl.when(pred)
            def _():
                arrived(rs.at[g, t], d_r.at[g, t], do_s.at[0, t], inward)
                add(g, t, g)

            send(yp.at[g, t], rs.at[slot, t], s.at[j, t], d_r.at[slot, t], dev, pred)

    def home(src, e, k, pred=None):
        for r in range(3):
            there = lax.rem(d + r + 1, 4)
            send(src.at[:, there], fin.at[e, :, :, own_at], e_s.at[k, r], e_r.at[k, r], dp_dev[r], pred)

        def own():
            fin[e, :, :, own_at] = src[:, d]

        if pred is None:
            own()
        else:
            pl.when(pred)(own)

    def finish(pred, both):
        @pl.when(pred)
        def _():
            for t in range(2):
                arrived(rs.at[z, t], d_r.at[z, t], do_s.at[0, t], inward)
                add(z, t, z)
                if both:
                    arrived(rs.at[8, t], d_r.at[8, t], do_s.at[0, t], outward)
                    add(z, t, 8)

        home(yp.at[z], half, 0, pred)

    for j in range(8):
        front(j)
        if j >= 1:
            middle(j - 1)
        if j >= 2:
            back(j - 2)
    chain(1, is_inner, di_s, inward)
    finish(is_inner, True)
    middle(7)

    send(act.at[low], act_in.at[low], sh_s.at[0], sh_r.at[0], sec_next, sx == 3)
    send(cot.at[low], cot_in.at[low], sh_s.at[2], sh_r.at[2], sec_prev, sx == 0)

    @pl.when(is_via)
    def _():
        arrived(via_in, sh_r.at[6], sh_s.at[6], sec_skip)

    send(via_in, via_out, sh_s.at[6], sh_r.at[7], sec_over, is_via)

    back(6)
    chain(3, is_inner, di_s, inward)
    chain(2, is_inner, do_s, outward)
    back(7)
    chain(6, is_inner, di_s, inward)
    chain(4, is_inner, do_s, outward)
    finish(is_edge, False)
    chain(1, is_edge, do_s, beyond, 9)
    chain(7, is_inner, di_s, inward)
    chain(5, is_inner, do_s, outward)
    chain(2, is_edge, do_s, outward, 9)

    h_all = ag[...].reshape(8 * rows, 3 * hidden)
    x_all = xg[:, 0].reshape(8 * rows, chunk)
    dw_mine[:, : 2 * hidden] = dot(x_all, h_all[:, : 2 * hidden], 0, 0)
    g_all = xg[:, 1].reshape(8 * rows, chunk)
    dw_mine[:, 2 * hidden :] = dot(g_all, h_all[:, 2 * hidden :], 0, 0)
    for k in range(3):
        at = pl.ds(pl.multiple_of(hidden * k + (1 - c) * cols, cols), cols)
        dw_send[k] = dw_mine[:, at].astype(BF16)
        send(dw_send.at[k], dw_in.at[k], q_s.at[k], q_r.at[k], sibling)

    def leave(e, k):
        for r in range(3):
            there = lax.rem(d + 3 - r, 4)
            at = pl.ds(pl.multiple_of(there * chunk, 128), chunk)
            arrived(fin.at[e, :, :, at], e_r.at[k, r], e_s.at[k, r], dp_dev[r])
        at = pl.ds(pl.multiple_of(e * CAP, CAP), CAP)
        pick_half = e == 0
        gate = jnp.where(pick_half, slot_gates[:CAP], slot_gates[CAP:])
        root = jnp.where(pick_half, inv_root[:CAP], inv_root[CAP:])
        ysend[at] = (gate * fin[e, 0].astype(F32)).astype(BF16)
        send(ysend.at[at], yin.at[at], x_s.at[0, k], x_r.at[0, k], sec_next)
        d_rows = fin[e, 1].astype(F32)
        n_rows = normed[at]
        spread = jnp.mean(n_rows * d_rows, axis=1, keepdims=True)
        dsend[at] = (root * (d_rows - n_rows * spread)).astype(BF16)
        send(dsend.at[at], din.at[at], x_s.at[1, k], x_r.at[1, k], sec_prev)

    leave(half, 0)

    @pl.when(is_via)
    def _():
        arrived(via_out, sh_r.at[7], sh_s.at[7], sec_over)

    send(via_out, act_in.at[high], sh_s.at[7], sh_r.at[1], sec_prev, sx == 1)
    send(via_out, cot_in.at[high], sh_s.at[7], sh_r.at[3], sec_next, sx == 2)

    for t in range(2):
        arrived(rs.at[9, t], d_r.at[9, t], do_s.at[0, t], outward)
    home(rs.at[9], 1 - half, 1)
    leave(1 - half, 1)

    for k, out in enumerate((d_gate_out, d_up_out, d_down_out)):
        arrived(dw_in.at[k], q_r.at[k], q_s.at[k], sibling)
        at = pl.ds(pl.multiple_of(hidden * k + c * cols, cols), cols)
        out[...] = (dw_mine[:, at] + dw_in[k].astype(F32)).astype(BF16)

    for t, (out, kept, pick, extra, dev) in enumerate(
        ((next_act, act_in, pick_prev, yin, sec_next), (prev_grad, cot_in, pick_next, din, sec_prev))
    ):
        arrived(pick, sh_r.at[4 + t], sh_s.at[4 + t], dev)
        arrived(kept.at[low], sh_r.at[2 * t], sh_s.at[2 * t], dev)
        arrived(kept.at[high], sh_r.at[2 * t + 1], sh_s.at[2 * t + 1], dev)
        for k, e in ((0, half), (1, 1 - half)):
            at = pl.ds(pl.multiple_of(e * CAP, CAP), CAP)
            arrived(extra.at[at], x_r.at[t, k], x_s.at[t, k], dev)
        out[...] = (kept[...].astype(F32) + dot(pick[...], extra[...], 0, 0)).astype(BF16)

    for pred, build in pending:
        if pred is None:
            build().wait_send()
        else:
            pl.when(pred)(lambda build=build: build().wait_send())


def per_device(act, cotangent, expert_ids, gate_values, w_gate, w_up, w_down_t):
    tokens, width = act.shape[1:]
    depth, cols = w_gate.shape[1:]
    chunk, hidden = width // 4, 2 * cols
    vmem = pl.BlockSpec(memory_space=pltpu.VMEM)
    anywhere = pl.BlockSpec(memory_space=pltpu.HBM)
    dma = pltpu.SemaphoreType.DMA
    slots = EXPERTS * CAP
    topk = expert_ids.shape[2]
    outs = pl.pallas_call(
        kernel,
        name="moe_relay",
        out_shape=[
            jax.ShapeDtypeStruct((tokens, width), BF16),
            jax.ShapeDtypeStruct((tokens, width), BF16),
            jax.ShapeDtypeStruct((depth, cols), BF16),
            jax.ShapeDtypeStruct((depth, cols), BF16),
            jax.ShapeDtypeStruct((depth, cols), BF16),
        ],
        in_specs=[anywhere] * 7,
        out_specs=[vmem] * 5,
        scratch_shapes=[
            pltpu.VMEM((tokens, width), BF16),
            pltpu.VMEM((tokens, width), BF16),
            pltpu.VMEM((topk, tokens), jnp.int32),
            pltpu.VMEM((topk, tokens), F32),
            pltpu.VMEM((depth, 3 * hidden), BF16),
            pltpu.VMEM((EXPERTS, 2, CAP, width), BF16),
            pltpu.VMEM((EXPERTS, 2, 4, CAP, chunk), BF16),
            pltpu.VMEM((8, 2, 4, CAP, chunk), BF16),
            pltpu.VMEM((slots, tokens), BF16),
            pltpu.VMEM((slots, tokens), BF16),
            pltpu.VMEM((slots, tokens), BF16),
            pltpu.VMEM((tokens, width), BF16),
            pltpu.VMEM((tokens, width), BF16),
            pltpu.VMEM((tokens // 2, width), BF16),
            pltpu.VMEM((tokens // 2, width), BF16),
            pltpu.VMEM((slots, width), F32),
            pltpu.VMEM((8, 4, CAP, 3 * hidden), BF16),
            pltpu.VMEM((8, 4, CAP, 3 * hidden), F32),
            pltpu.VMEM((8, 3, CAP, 3 * hidden), BF16),
            pltpu.VMEM((8, 4, CAP, 3 * hidden), BF16),
            pltpu.VMEM((8, 2, 4, CAP, chunk), BF16),
            pltpu.VMEM((10, 2, 4, CAP, chunk), BF16),
            pltpu.VMEM((EXPERTS, 2, CAP, width), BF16),
            pltpu.VMEM((slots, width), BF16),
            pltpu.VMEM((slots, width), BF16),
            pltpu.VMEM((slots, width), BF16),
            pltpu.VMEM((slots, width), BF16),
            pltpu.VMEM((depth, 3 * hidden), F32),
            pltpu.VMEM((3, depth, cols), BF16),
            pltpu.VMEM((3, depth, cols), BF16),
            dma((7,)),
            dma((3,)), dma((3,)),
            dma((3,)), dma((3,)),
            dma((8,)), dma((8,)),
            dma((8, 2)), dma((9, 2)), dma((8, 2)),
            dma((8, 3)), dma((8, 3)),
            dma((8, 3)), dma((8, 3)),
            dma((8, 2)), dma((8, 2)), dma((10, 2)),
            dma((2, 3)), dma((2, 3)),
            dma((2, 2)), dma((2, 2)),
            dma((3,)), dma((3,)),
        ],
        compiler_params=pltpu.CompilerParams(
            collective_id=0, has_side_effects=True, vmem_limit_bytes=50 * 2**20
        ),
    )(
        act[0],
        cotangent[0],
        jnp.swapaxes(expert_ids[0], 0, 1),
        jnp.swapaxes(gate_values[0], 0, 1),
        w_gate[0],
        w_up[0],
        w_down_t[0],
    )
    return tuple(out[None] for out in outs)


def solution(mesh):
    rows = P("section", ("expert", "dp"), None)
    weights = P("section", "dp", "expert")
    return jax.shard_map(
        per_device,
        mesh=mesh,
        in_specs=(rows,) * 4 + (weights,) * 3,
        out_specs=(rows,) * 2 + (weights,) * 3,
        check_vma=False,
    )
```

```python
import jax
import jax.numpy as jnp
from jax import lax
from jax.experimental import pallas as pl
from jax.experimental.pallas import tpu as pltpu
from jax.sharding import PartitionSpec as P

MESH = pl.DeviceIdType.MESH
EXPERTS = 2
CAP = 16
VIA = 5
F32 = jnp.float32
BF16 = jnp.bfloat16


def dot(left, right, left_dim, right_dim, precision=None):
    return lax.dot_general(
        left,
        right,
        (((left_dim,), (right_dim,)), ((), ())),
        preferred_element_type=F32,
        precision=precision,
    )


def kernel(
    act_h, cot_h, ids_h, gates_h, w_gate, w_up, w_down,
    next_act, prev_grad, d_gate_out, d_up_out, d_down_out,
    act, cot, ids, gates,
    wf, pk, rb, xg, picks, pick_prev, pick_next, act_in, cot_in, via_in, via_out,
    normed, hp, hf, hr, hs, ht, ag, yp, rs, fin, ysend, dsend, yin, din, dw_mine, dw_send, dw_in,
    l_s, w_s, w_r, a_s, a_r, sh_s, sh_r, v_s, v_r, bi_s, bo_s, b_r, p_s, p_r, g_s, g_r,
    di_s, do_s, d_r, e_s, e_r, x_s, x_r, q_s, q_r,
):
    sec, ex, d = lax.axis_index("section"), lax.axis_index("expert"), lax.axis_index("dp")
    z, c = ex // 2, ex % 2
    q, half = z % 4, z // 4
    sx, sy = sec % 4, sec // 4
    sgn = 1 - 2 * (q // 2)
    qm = q * (1 - q // 2) + (3 - q) * (q // 2)
    edge = 1 - qm
    is_edge, is_inner = qm == 0, qm == 1
    width = act.shape[1]
    chunk = width // 4
    cols = w_gate.shape[1]

    def z_dev(step):
        return {"expert": lax.rem(z + step + 8, 8) * 2 + c}

    inward, outward, beyond = z_dev(sgn), z_dev(-sgn), z_dev(-2 * sgn)
    sibling = {"expert": z * 2 + 1 - c}
    lo, hi = d % 2, d // 2
    dp_near, dp_far = {"dp": d + 1 - 2 * lo}, {"dp": lax.rem(d + 2, 4)}
    dp_dev = [{"dp": lax.rem(d + r + 1, 4)} for r in range(3)]
    sec_next = {"section": lax.rem(sec + 1, 8)}
    sec_prev = {"section": lax.rem(sec + 7, 8)}
    sec_skip = {"section": sy * 4 + lax.rem(sx + 2, 4)}
    sec_over = {"section": lax.rem(sec + 4, 8)}

    def fetch(src, dst, k):
        copy = pltpu.make_async_copy(src, dst, l_s.at[k])
        copy.start()
        return copy

    small = [fetch(ids_h, ids, 0), fetch(gates_h, gates, 1)]
    big = [fetch(act_h, act, 2), fetch(cot_h, cot, 3)]
    weights = []
    for k, w in enumerate((w_gate, w_up, w_down)):
        at = pl.ds(pl.multiple_of(2 * cols * k + c * cols, cols), cols)
        weights.append(fetch(w, wf.at[:, at], 4 + k))

    bar = pltpu.get_barrier_semaphore()
    partners = (inward, outward, beyond, sibling, *dp_dev, sec_next, sec_prev, sec_skip, sec_over)
    for dev in partners:
        pl.semaphore_signal(bar, inc=1, device_id=dev, device_id_type=MESH)

    for copy in small:
        copy.wait()
    tokens = act.shape[0]
    upper = (
        lax.broadcasted_iota(jnp.int32, (tokens, tokens), 0)
        <= lax.broadcasted_iota(jnp.int32, (tokens, tokens), 1)
    ).astype(BF16)
    slots = lax.broadcasted_iota(jnp.int32, (CAP, tokens), 0).astype(F32)
    slot_gate = []
    for e in range(EXPERTS):
        named = jnp.where(ids[...] == e, 1.0, 0.0)
        gate_of = jnp.sum(named * gates[...], axis=0, keepdims=True)
        routed = jnp.sum(named, axis=0, keepdims=True)
        within = dot(jnp.broadcast_to(routed, (8, tokens)).astype(BF16), upper, 1, 0)[0:1] - 1.0
        pick = jnp.where((slots == within) & (routed > 0.5), 1.0, 0.0)
        slot_gate.append(jnp.sum(pick * gate_of, axis=1, keepdims=True))
        picks[e * CAP : (e + 1) * CAP] = pick.astype(BF16)
    slot_gates = jnp.concatenate(slot_gate, axis=0)
    for copy in big:
        copy.wait()
    x_rows = dot(picks[...], act[...], 1, 0)
    inv_root = lax.rsqrt(jnp.mean(x_rows * x_rows, axis=1, keepdims=True) + 1e-6)
    x_rows = x_rows * inv_root
    normed[...] = x_rows
    x_rows = x_rows.astype(BF16)
    g_rows = (slot_gates * dot(picks[...], cot[...], 1, 0)).astype(BF16)
    for e in range(EXPERTS):
        pk[e, 0] = x_rows[e * CAP : (e + 1) * CAP]
        pk[e, 1] = g_rows[e * CAP : (e + 1) * CAP]
    for copy in weights:
        copy.wait()

    pl.semaphore_wait(bar, len(partners))

    pending = []

    def make(src, dst, s, r, dev):
        return pltpu.make_async_remote_copy(
            src_ref=src, dst_ref=dst, send_sem=s, recv_sem=r, device_id=dev, device_id_type=MESH
        )

    def send(src, dst, s, r, dev, pred=None):
        def build():
            return make(src, dst, s, r, dev)

        if pred is None:
            build().start()
        else:
            pl.when(pred)(lambda: build().start())
        pending.append((pred, build))

    def arrived(dst, r, s, dev):
        make(dst, dst, s, r, dev).wait_recv()

    at_edge, at_inner = (0, -2, -1, 1, 2, 3, 5, 4), (0, 1, -1, 2, -3, -2, 4, 3)
    group = [lax.rem(z + sgn * (i + edge * (o - i)) + 16, 8) for o, i in zip(at_edge, at_inner)]

    both = ((hi, 1 - lo), (1 - hi, lo), (1 - hi, 1 - lo))
    for r, (pair_of, place) in enumerate(both):
        there = 2 * pair_of + place
        at = pl.ds(pl.multiple_of(there * chunk, 128), chunk)
        send(pk.at[:, :, :, at], rb.at[:, hi, :, lo], a_s.at[r], a_r.at[r], {"dp": there})
    own_at = pl.ds(pl.multiple_of(d * chunk, 128), chunk)
    for e in range(EXPERTS):
        for t in range(2):
            rb[e, hi, t, lo] = pk[e, t, :, own_at]
    for k, w in enumerate((w_gate, w_up, w_down)):
        at = pl.ds(pl.multiple_of(2 * cols * k + c * cols, cols), cols)
        send(w, wf.at[:, at], w_s.at[k], w_r.at[k], sibling)

    reach = z_dev(-sgn * (1 + qm))

    def set_out(p):
        pair_of = hi if p == 0 else 1 - hi
        send(rb.at[1 - half, pair_of], xg.at[z, pair_of], bo_s.at[8, p], b_r.at[z, p], reach)
        send(rb.at[half, pair_of], xg.at[z, pair_of], bi_s.at[0, p], b_r.at[z, p], inward)
        send(rb.at[half, pair_of], xg.at[z, pair_of], bo_s.at[0, p], b_r.at[z, p], outward, is_inner)

    arrived(rb.at[:, hi, :, 1 - lo], a_r.at[0], a_s.at[0], dp_near)
    set_out(0)
    for r in (1, 2):
        pair_of, place = both[r]
        arrived(rb.at[:, pair_of, :, place], a_r.at[r], a_s.at[r], {"dp": 2 * pair_of + place})
    set_out(1)

    piece = CAP
    mid = tokens - VIA * piece
    low, high = pl.ds(0, mid), pl.ds(mid, VIA * piece)
    parts = [pl.ds(mid + k * piece, piece) for k in range(VIA)]
    send(picks, pick_prev, sh_s.at[4], sh_r.at[4], sec_next)
    send(picks, pick_next, sh_s.at[5], sh_r.at[5], sec_prev)
    send(act.at[high], via_in, sh_s.at[1], sh_r.at[6], sec_skip, sx == 3)
    send(cot.at[high], via_in, sh_s.at[3], sh_r.at[6], sec_skip, sx == 0)
    send(act.at[low], act_in.at[low], sh_s.at[0], sh_r.at[0], sec_next, sx != 3)
    send(cot.at[low], cot_in.at[low], sh_s.at[2], sh_r.at[2], sec_prev, sx != 0)
    for k, part in enumerate(parts):
        send(act.at[part], act_in.at[part], v_s.at[0, k], v_r.at[0, k], sec_next, sx != 3)
        send(cot.at[part], cot_in.at[part], v_s.at[1, k], v_r.at[1, k], sec_prev, sx != 0)
    is_via = (sx == 1) | (sx == 2)

    xg[z] = rb[half]
    for k in range(3):
        at = pl.ds(pl.multiple_of(2 * cols * k + (1 - c) * cols, cols), cols)
        arrived(wf.at[:, at], w_r.at[k], w_s.at[k], sibling)

    hidden = 2 * cols
    rows = 4 * CAP

    def receive(j, p):
        g = group[j]
        pair_of = hi if p == 0 else 1 - hi
        piece_of = xg.at[g, pair_of]
        if j > 0:
            arrived(piece_of, b_r.at[g, p], bo_s.at[0, p], inward)
        if j in (1, 2):
            send(piece_of, piece_of, bi_s.at[j, p], b_r.at[g, p], inward, is_edge)
        if j in (1, 3, 6, 7):
            send(piece_of, piece_of, bo_s.at[j, p], b_r.at[g, p], outward, is_inner)
        if j in (2, 4, 5):
            send(piece_of, piece_of, bi_s.at[j, p], b_r.at[g, p], inward, is_inner)

    def front(j):
        g = group[j]
        x = xg[g, :, 0].reshape(rows, chunk)
        gr = xg[g, :, 1].reshape(rows, chunk)
        hf[j] = jnp.concatenate(
            [dot(x, wf[:, : 2 * hidden], 1, 0), dot(gr, wf[:, 2 * hidden :], 1, 0)], axis=1
        ).reshape(2, 2, CAP, 3 * hidden)
        hp[j] = hf[j, :, 1 - lo].astype(BF16)
        send(hp.at[j], hr.at[j], p_s.at[j, 0], p_r.at[j, 0], dp_near)

    def pair(j):
        arrived(hr.at[j], p_r.at[j, 0], p_s.at[j, 0], dp_near)
        hs[j] = (hf[j, 1 - hi, lo] + hr[j, 1 - hi].astype(F32)).astype(BF16)
        send(hs.at[j], ht.at[j], p_s.at[j, 1], p_r.at[j, 1], dp_far)

    def middle(j):
        g = group[j]
        total = hf[j, hi, lo] + hr[j, hi].astype(F32)
        arrived(ht.at[j], p_r.at[j, 1], p_s.at[j, 1], dp_far)
        total = total + ht[j].astype(F32)
        pre_gate = total[:, :hidden]
        pre_up = total[:, hidden : 2 * hidden]
        hidden_grad = total[:, 2 * hidden :]
        sig = jax.nn.sigmoid(pre_gate)
        silu = pre_gate * sig
        ag[g, hi, lo, :, :hidden] = (hidden_grad * pre_up * sig * (1.0 + pre_gate * (1.0 - sig))).astype(BF16)
        ag[g, hi, lo, :, hidden : 2 * hidden] = (hidden_grad * silu).astype(BF16)
        ag[g, hi, lo, :, 2 * hidden :] = (silu * pre_up).astype(BF16)
        send(ag.at[g, hi, lo], ag.at[g, hi, lo], g_s.at[j, 0], g_r.at[j, 0], dp_far)

    def spread_out(j):
        g = group[j]
        arrived(ag.at[g, 1 - hi, lo], g_r.at[j, 0], g_s.at[j, 0], dp_far)
        send(ag.at[g, :, lo], ag.at[g, :, lo], g_s.at[j, 1], g_r.at[j, 1], dp_near)

    def back(j):
        g = group[j]
        arrived(ag.at[g, :, 1 - lo], g_r.at[j, 1], g_s.at[j, 1], dp_near)
        h = ag[g].reshape(rows, 3 * hidden)
        slot = 8 if j == 3 else g
        for t, (a, b) in enumerate(((2 * hidden, 3 * hidden), (0, 2 * hidden))):
            yp[g, t] = dot(h[:, a:b], wf[:, a:b], 1, 1).astype(BF16).reshape(4, CAP, chunk)
            if j >= 3:
                send(yp.at[g, t], rs.at[slot, t], di_s.at[j, t], d_r.at[slot, t], inward, is_edge)

    def cross():
        send(act.at[low], act_in.at[low], sh_s.at[0], sh_r.at[0], sec_next, sx == 3)
        send(cot.at[low], cot_in.at[low], sh_s.at[2], sh_r.at[2], sec_prev, sx == 0)

        @pl.when(is_via)
        def _():
            arrived(via_in, sh_r.at[6], sh_s.at[6], sec_skip)

        for k in range(VIA):
            at = pl.ds(k * piece, piece)
            send(via_in.at[at], via_out.at[at], v_s.at[2, k], v_r.at[2, k], sec_over, is_via)

    def pass_on(k):
        at = pl.ds(k * piece, piece)

        @pl.when(is_via)
        def _():
            arrived(via_out.at[at], v_r.at[2, k], v_s.at[2, k], sec_over)

        send(via_out.at[at], act_in.at[parts[k]], v_s.at[3, k], v_r.at[0, k], sec_prev, sx == 1)
        send(via_out.at[at], cot_in.at[parts[k]], v_s.at[3, k], v_r.at[1, k], sec_next, sx == 2)

    def add(g, t, slot):
        yp[g, t] = (yp[g, t].astype(F32) + rs[slot, t].astype(F32)).astype(BF16)

    def chain(j, pred, s, dev, slot=None):
        g = group[j]
        slot = g if slot is None else slot
        for t in range(2):

            @pl.when(pred)
            def _():
                arrived(rs.at[g, t], d_r.at[g, t], do_s.at[0, t], inward)
                add(g, t, g)

            send(yp.at[g, t], rs.at[slot, t], s.at[j, t], d_r.at[slot, t], dev, pred)

    def home(src, e, k, pred=None):
        for r in range(3):
            there = lax.rem(d + r + 1, 4)
            send(src.at[:, there], fin.at[e, :, :, own_at], e_s.at[k, r], e_r.at[k, r], dp_dev[r], pred)

        def own():
            fin[e, :, :, own_at] = src[:, d]

        if pred is None:
            own()
        else:
            pl.when(pred)(own)

    def finish(pred, both):
        @pl.when(pred)
        def _():
            for t in range(2):
                arrived(rs.at[z, t], d_r.at[z, t], do_s.at[0, t], inward)
                add(z, t, z)
                if both:
                    arrived(rs.at[8, t], d_r.at[8, t], do_s.at[0, t], outward)
                    add(z, t, 8)

        home(yp.at[z], half, 0, pred)

    for j in range(8):
        receive(j, 0)
        receive(j, 1)
        front(j)
        if j >= 1:
            pair(j - 1)
        if j >= 2:
            middle(j - 2)
        if j >= 3:
            spread_out(j - 3)
        if j >= 4:
            back(j - 4)
    pair(7)
    middle(6)
    spread_out(5)
    back(4)
    middle(7)
    spread_out(6)
    back(5)
    chain(1, is_inner, di_s, inward)
    spread_out(7)
    finish(is_inner, True)
    back(6)
    chain(3, is_inner, di_s, inward)
    chain(2, is_inner, do_s, outward)
    back(7)
    chain(6, is_inner, di_s, inward)
    cross()
    chain(4, is_inner, do_s, outward)
    finish(is_edge, False)
    chain(1, is_edge, do_s, beyond, 9)
    chain(7, is_inner, di_s, inward)
    chain(5, is_inner, do_s, outward)
    chain(2, is_edge, do_s, outward, 9)

    pass_on(0)
    pass_on(1)
    h_all = ag[...].reshape(8 * rows, 3 * hidden)
    x_all = xg[:, :, 0].reshape(8 * rows, chunk)
    dw_mine[:, : 2 * hidden] = dot(x_all, h_all[:, : 2 * hidden], 0, 0)
    g_all = xg[:, :, 1].reshape(8 * rows, chunk)
    dw_mine[:, 2 * hidden :] = dot(g_all, h_all[:, 2 * hidden :], 0, 0)
    for k in range(3):
        at = pl.ds(pl.multiple_of(hidden * k + (1 - c) * cols, cols), cols)
        dw_send[k] = dw_mine[:, at].astype(BF16)
        send(dw_send.at[k], dw_in.at[k], q_s.at[k], q_r.at[k], sibling)

    def leave(e, k):
        for r in range(3):
            there = lax.rem(d + 3 - r, 4)
            at = pl.ds(pl.multiple_of(there * chunk, 128), chunk)
            arrived(fin.at[e, :, :, at], e_r.at[k, r], e_s.at[k, r], dp_dev[r])
        at = pl.ds(pl.multiple_of(e * CAP, CAP), CAP)
        pick_half = e == 0
        gate = jnp.where(pick_half, slot_gates[:CAP], slot_gates[CAP:])
        root = jnp.where(pick_half, inv_root[:CAP], inv_root[CAP:])
        ysend[at] = (gate * fin[e, 0].astype(F32)).astype(BF16)
        send(ysend.at[at], yin.at[at], x_s.at[0, k], x_r.at[0, k], sec_next)
        d_rows = fin[e, 1].astype(F32)
        n_rows = normed[at]
        spread = jnp.mean(n_rows * d_rows, axis=1, keepdims=True)
        dsend[at] = (root * (d_rows - n_rows * spread)).astype(BF16)
        send(dsend.at[at], din.at[at], x_s.at[1, k], x_r.at[1, k], sec_prev)

    for k in range(2, VIA):
        pass_on(k)
    leave(half, 0)

    for t in range(2):
        arrived(rs.at[9, t], d_r.at[9, t], do_s.at[0, t], outward)
    home(rs.at[9], 1 - half, 1)
    leave(1 - half, 1)

    for k, out in enumerate((d_gate_out, d_up_out, d_down_out)):
        arrived(dw_in.at[k], q_r.at[k], q_s.at[k], sibling)
        at = pl.ds(pl.multiple_of(hidden * k + c * cols, cols), cols)
        out[...] = (dw_mine[:, at] + dw_in[k].astype(F32)).astype(BF16)

    for t, (out, kept, pick, extra, dev) in enumerate(
        ((next_act, act_in, pick_prev, yin, sec_next), (prev_grad, cot_in, pick_next, din, sec_prev))
    ):
        arrived(pick, sh_r.at[4 + t], sh_s.at[4 + t], dev)
        arrived(kept.at[low], sh_r.at[2 * t], sh_s.at[2 * t], dev)
        for k, part in enumerate(parts):
            arrived(kept.at[part], v_r.at[t, k], v_s.at[t, k], dev)
        for k, e in ((0, half), (1, 1 - half)):
            at = pl.ds(pl.multiple_of(e * CAP, CAP), CAP)
            arrived(extra.at[at], x_r.at[t, k], x_s.at[t, k], dev)
        out[...] = (kept[...].astype(F32) + dot(pick[...], extra[...], 0, 0)).astype(BF16)

    for pred, build in pending:
        if pred is None:
            build().wait_send()
        else:
            pl.when(pred)(lambda build=build: build().wait_send())


def per_device(act, cotangent, expert_ids, gate_values, w_gate, w_up, w_down_t):
    tokens, width = act.shape[1:]
    depth, cols = w_gate.shape[1:]
    chunk, hidden = width // 4, 2 * cols
    vmem = pl.BlockSpec(memory_space=pltpu.VMEM)
    anywhere = pl.BlockSpec(memory_space=pltpu.HBM)
    dma = pltpu.SemaphoreType.DMA
    slots = EXPERTS * CAP
    topk = expert_ids.shape[2]
    outs = pl.pallas_call(
        kernel,
        name="moe_relay",
        out_shape=[
            jax.ShapeDtypeStruct((tokens, width), BF16),
            jax.ShapeDtypeStruct((tokens, width), BF16),
            jax.ShapeDtypeStruct((depth, cols), BF16),
            jax.ShapeDtypeStruct((depth, cols), BF16),
            jax.ShapeDtypeStruct((depth, cols), BF16),
        ],
        in_specs=[anywhere] * 7,
        out_specs=[vmem] * 5,
        scratch_shapes=[
            pltpu.VMEM((tokens, width), BF16),
            pltpu.VMEM((tokens, width), BF16),
            pltpu.VMEM((topk, tokens), jnp.int32),
            pltpu.VMEM((topk, tokens), F32),
            pltpu.VMEM((depth, 3 * hidden), BF16),
            pltpu.VMEM((EXPERTS, 2, CAP, width), BF16),
            pltpu.VMEM((EXPERTS, 2, 2, 2, CAP, chunk), BF16),
            pltpu.VMEM((8, 2, 2, 2, CAP, chunk), BF16),
            pltpu.VMEM((slots, tokens), BF16),
            pltpu.VMEM((slots, tokens), BF16),
            pltpu.VMEM((slots, tokens), BF16),
            pltpu.VMEM((tokens, width), BF16),
            pltpu.VMEM((tokens, width), BF16),
            pltpu.VMEM((VIA * CAP, width), BF16),
            pltpu.VMEM((VIA * CAP, width), BF16),
            pltpu.VMEM((slots, width), F32),
            pltpu.VMEM((8, 2, CAP, 3 * hidden), BF16),
            pltpu.VMEM((8, 2, 2, CAP, 3 * hidden), F32),
            pltpu.VMEM((8, 2, CAP, 3 * hidden), BF16),
            pltpu.VMEM((8, CAP, 3 * hidden), BF16),
            pltpu.VMEM((8, CAP, 3 * hidden), BF16),
            pltpu.VMEM((8, 2, 2, CAP, 3 * hidden), BF16),
            pltpu.VMEM((8, 2, 4, CAP, chunk), BF16),
            pltpu.VMEM((10, 2, 4, CAP, chunk), BF16),
            pltpu.VMEM((EXPERTS, 2, CAP, width), BF16),
            pltpu.VMEM((slots, width), BF16),
            pltpu.VMEM((slots, width), BF16),
            pltpu.VMEM((slots, width), BF16),
            pltpu.VMEM((slots, width), BF16),
            pltpu.VMEM((depth, 3 * hidden), F32),
            pltpu.VMEM((3, depth, cols), BF16),
            pltpu.VMEM((3, depth, cols), BF16),
            dma((7,)),
            dma((3,)), dma((3,)),
            dma((3,)), dma((3,)),
            dma((7,)), dma((7,)),
            dma((4, VIA)), dma((3, VIA)),
            dma((8, 2)), dma((9, 2)), dma((8, 2)),
            dma((8, 2)), dma((8, 2)),
            dma((8, 2)), dma((8, 2)),
            dma((8, 2)), dma((8, 2)), dma((10, 2)),
            dma((2, 3)), dma((2, 3)),
            dma((2, 2)), dma((2, 2)),
            dma((3,)), dma((3,)),
        ],
        compiler_params=pltpu.CompilerParams(
            collective_id=0, has_side_effects=True, vmem_limit_bytes=62 * 2**20
        ),
    )(
        act[0],
        cotangent[0],
        jnp.swapaxes(expert_ids[0], 0, 1),
        jnp.swapaxes(gate_values[0], 0, 1),
        w_gate[0],
        w_up[0],
        w_down_t[0],
    )
    return tuple(out[None] for out in outs)


def solution(mesh):
    rows = P("section", ("expert", "dp"), None)
    weights = P("section", "dp", "expert")
    return jax.shard_map(
        per_device,
        mesh=mesh,
        in_specs=(rows,) * 4 + (weights,) * 3,
        out_specs=(rows,) * 2 + (weights,) * 3,
        check_vma=False,
    )
```

```python
import jax
import jax.numpy as jnp
from jax import lax
from jax.experimental import pallas as pl
from jax.experimental.pallas import tpu as pltpu
from jax.sharding import PartitionSpec as P

MESH = pl.DeviceIdType.MESH
EXPERTS = 2
CAP = 16
VIA = 5
F32 = jnp.float32
BF16 = jnp.bfloat16


def dot(left, right, left_dim, right_dim, precision=None):
    return lax.dot_general(
        left,
        right,
        (((left_dim,), (right_dim,)), ((), ())),
        preferred_element_type=F32,
        precision=precision,
    )


def kernel(
    act_h, cot_h, ids_h, gates_h, w_gate, w_up, w_down,
    next_act, prev_grad, d_gate_out, d_up_out, d_down_out,
    act, cot, ids, gates,
    wf, pk, rb, xg, picks, pick_prev, pick_next, act_in, cot_in, via_in, via_out,
    normed, hp, hf, hr, hs, ht, ag, yp, rs, fin, ysend, dsend, yin, din, dw_mine, dw_send, dw_in,
    l_s, w_s, w_r, a_s, a_r, sh_s, sh_r, v_s, v_r, bi_s, bo_s, b_r, p_s, p_r, g_s, g_r,
    di_s, do_s, d_r, e_s, e_r, x_s, x_r, q_s, q_r,
):
    sec, ex, d = lax.axis_index("section"), lax.axis_index("expert"), lax.axis_index("dp")
    z, c = ex // 2, ex % 2
    q, half = z % 4, z // 4
    sx, sy = sec % 4, sec // 4
    sgn = 1 - 2 * (q // 2)
    qm = q * (1 - q // 2) + (3 - q) * (q // 2)
    edge = 1 - qm
    is_edge, is_inner = qm == 0, qm == 1
    width = act.shape[1]
    chunk = width // 4
    cols = w_gate.shape[1]

    def z_dev(step):
        return {"expert": lax.rem(z + step + 8, 8) * 2 + c}

    inward, outward, beyond = z_dev(sgn), z_dev(-sgn), z_dev(-2 * sgn)
    sibling = {"expert": z * 2 + 1 - c}
    lo, hi = d % 2, d // 2
    dp_near, dp_far = {"dp": d + 1 - 2 * lo}, {"dp": lax.rem(d + 2, 4)}
    dp_dev = [{"dp": lax.rem(d + r + 1, 4)} for r in range(3)]
    sec_next = {"section": lax.rem(sec + 1, 8)}
    sec_prev = {"section": lax.rem(sec + 7, 8)}
    sec_skip = {"section": sy * 4 + lax.rem(sx + 2, 4)}
    sec_over = {"section": lax.rem(sec + 4, 8)}

    def fetch(src, dst, k):
        copy = pltpu.make_async_copy(src, dst, l_s.at[k])
        copy.start()
        return copy

    small = [fetch(ids_h, ids, 0), fetch(gates_h, gates, 1)]
    big = [fetch(act_h, act, 2), fetch(cot_h, cot, 3)]
    weights = []
    for k, w in enumerate((w_gate, w_up, w_down)):
        at = pl.ds(pl.multiple_of(2 * cols * k + c * cols, cols), cols)
        weights.append(fetch(w, wf.at[:, at], 4 + k))

    bar = pltpu.get_barrier_semaphore()
    partners = (inward, outward, beyond, sibling, *dp_dev, sec_next, sec_prev, sec_skip, sec_over)
    for dev in partners:
        pl.semaphore_signal(bar, inc=1, device_id=dev, device_id_type=MESH)

    for copy in small:
        copy.wait()
    tokens = act.shape[0]
    upper = (
        lax.broadcasted_iota(jnp.int32, (tokens, tokens), 0)
        <= lax.broadcasted_iota(jnp.int32, (tokens, tokens), 1)
    ).astype(BF16)
    slots = lax.broadcasted_iota(jnp.int32, (CAP, tokens), 0).astype(F32)
    slot_gate = []
    for e in range(EXPERTS):
        named = jnp.where(ids[...] == e, 1.0, 0.0)
        gate_of = jnp.sum(named * gates[...], axis=0, keepdims=True)
        routed = jnp.sum(named, axis=0, keepdims=True)
        within = dot(jnp.broadcast_to(routed, (8, tokens)).astype(BF16), upper, 1, 0)[0:1] - 1.0
        pick = jnp.where((slots == within) & (routed > 0.5), 1.0, 0.0)
        slot_gate.append(jnp.sum(pick * gate_of, axis=1, keepdims=True))
        picks[e * CAP : (e + 1) * CAP] = pick.astype(BF16)
    slot_gates = jnp.concatenate(slot_gate, axis=0)
    for copy in big:
        copy.wait()
    x_rows = dot(picks[...], act[...], 1, 0)
    inv_root = lax.rsqrt(jnp.mean(x_rows * x_rows, axis=1, keepdims=True) + 1e-6)
    x_rows = x_rows * inv_root
    normed[...] = x_rows
    x_rows = x_rows.astype(BF16)
    g_rows = (slot_gates * dot(picks[...], cot[...], 1, 0)).astype(BF16)
    for e in range(EXPERTS):
        pk[e, 0] = x_rows[e * CAP : (e + 1) * CAP]
        pk[e, 1] = g_rows[e * CAP : (e + 1) * CAP]
    for copy in weights:
        copy.wait()

    pl.semaphore_wait(bar, len(partners))

    pending = []

    def make(src, dst, s, r, dev):
        return pltpu.make_async_remote_copy(
            src_ref=src, dst_ref=dst, send_sem=s, recv_sem=r, device_id=dev, device_id_type=MESH
        )

    def send(src, dst, s, r, dev, pred=None):
        def build():
            return make(src, dst, s, r, dev)

        if pred is None:
            build().start()
        else:
            pl.when(pred)(lambda: build().start())
        pending.append((pred, build))

    def arrived(dst, r, s, dev):
        make(dst, dst, s, r, dev).wait_recv()

    at_edge, at_inner = (0, -2, -1, 1, 2, 3, 5, 4), (0, 1, -1, 2, -3, -2, 4, 3)
    group = [lax.rem(z + sgn * (i + edge * (o - i)) + 16, 8) for o, i in zip(at_edge, at_inner)]

    both = ((hi, 1 - lo), (1 - hi, lo), (1 - hi, 1 - lo))
    for r, (pair_of, place) in enumerate(both):
        there = 2 * pair_of + place
        at = pl.ds(pl.multiple_of(there * chunk, 128), chunk)
        send(pk.at[:, :, :, at], rb.at[:, hi, :, lo], a_s.at[r], a_r.at[r], {"dp": there})
    own_at = pl.ds(pl.multiple_of(d * chunk, 128), chunk)
    for e in range(EXPERTS):
        for t in range(2):
            rb[e, hi, t, lo] = pk[e, t, :, own_at]
    for k, w in enumerate((w_gate, w_up, w_down)):
        at = pl.ds(pl.multiple_of(2 * cols * k + c * cols, cols), cols)
        send(w, wf.at[:, at], w_s.at[k], w_r.at[k], sibling)

    reach = z_dev(-sgn * (1 + qm))

    def set_out(p):
        pair_of = hi if p == 0 else 1 - hi
        send(rb.at[1 - half, pair_of], xg.at[z, pair_of], bo_s.at[8, p], b_r.at[z, p], reach)
        send(rb.at[half, pair_of], xg.at[z, pair_of], bi_s.at[0, p], b_r.at[z, p], inward)
        send(rb.at[half, pair_of], xg.at[z, pair_of], bo_s.at[0, p], b_r.at[z, p], outward, is_inner)

    arrived(rb.at[:, hi, :, 1 - lo], a_r.at[0], a_s.at[0], dp_near)
    set_out(0)
    for r in (1, 2):
        pair_of, place = both[r]
        arrived(rb.at[:, pair_of, :, place], a_r.at[r], a_s.at[r], {"dp": 2 * pair_of + place})
    set_out(1)

    piece = CAP
    mid = tokens - VIA * piece
    low, high = pl.ds(0, mid), pl.ds(mid, VIA * piece)
    parts = [pl.ds(mid + k * piece, piece) for k in range(VIA)]
    send(picks, pick_prev, sh_s.at[4], sh_r.at[4], sec_next)
    send(picks, pick_next, sh_s.at[5], sh_r.at[5], sec_prev)
    send(act.at[high], via_in, sh_s.at[1], sh_r.at[6], sec_skip, sx == 3)
    send(cot.at[high], via_in, sh_s.at[3], sh_r.at[6], sec_skip, sx == 0)
    send(act.at[low], act_in.at[low], sh_s.at[0], sh_r.at[0], sec_next, sx != 3)
    send(cot.at[low], cot_in.at[low], sh_s.at[2], sh_r.at[2], sec_prev, sx != 0)
    for k, part in enumerate(parts):
        send(act.at[part], act_in.at[part], v_s.at[0, k], v_r.at[0, k], sec_next, sx != 3)
        send(cot.at[part], cot_in.at[part], v_s.at[1, k], v_r.at[1, k], sec_prev, sx != 0)
    is_via = (sx == 1) | (sx == 2)

    xg[z] = rb[half]
    for k in range(3):
        at = pl.ds(pl.multiple_of(2 * cols * k + (1 - c) * cols, cols), cols)
        arrived(wf.at[:, at], w_r.at[k], w_s.at[k], sibling)

    hidden = 2 * cols
    rows = 4 * CAP

    def receive(j, p):
        g = group[j]
        pair_of = hi if p == 0 else 1 - hi
        piece_of = xg.at[g, pair_of]
        if j > 0:
            arrived(piece_of, b_r.at[g, p], bo_s.at[0, p], inward)
        if j in (1, 2):
            send(piece_of, piece_of, bi_s.at[j, p], b_r.at[g, p], inward, is_edge)
        if j in (1, 3, 6, 7):
            send(piece_of, piece_of, bo_s.at[j, p], b_r.at[g, p], outward, is_inner)
        if j in (2, 4, 5):
            send(piece_of, piece_of, bi_s.at[j, p], b_r.at[g, p], inward, is_inner)

    def front(j):
        g = group[j]
        x = xg[g, :, 0].reshape(rows, chunk)
        gr = xg[g, :, 1].reshape(rows, chunk)
        hf[j] = jnp.concatenate(
            [dot(x, wf[:, : 2 * hidden], 1, 0), dot(gr, wf[:, 2 * hidden :], 1, 0)], axis=1
        ).reshape(2, 2, CAP, 3 * hidden)
        hp[j] = hf[j, :, 1 - lo].astype(BF16)
        send(hp.at[j], hr.at[j], p_s.at[j, 0], p_r.at[j, 0], dp_near)

    def pair(j):
        arrived(hr.at[j], p_r.at[j, 0], p_s.at[j, 0], dp_near)
        hs[j] = (hf[j, 1 - hi, lo] + hr[j, 1 - hi].astype(F32)).astype(BF16)
        send(hs.at[j], ht.at[j], p_s.at[j, 1], p_r.at[j, 1], dp_far)

    def middle(j):
        g = group[j]
        total = hf[j, hi, lo] + hr[j, hi].astype(F32)
        arrived(ht.at[j], p_r.at[j, 1], p_s.at[j, 1], dp_far)
        total = total + ht[j].astype(F32)
        pre_gate = total[:, :hidden]
        pre_up = total[:, hidden : 2 * hidden]
        hidden_grad = total[:, 2 * hidden :]
        sig = jax.nn.sigmoid(pre_gate)
        silu = pre_gate * sig
        ag[g, hi, lo, :, :hidden] = (hidden_grad * pre_up * sig * (1.0 + pre_gate * (1.0 - sig))).astype(BF16)
        ag[g, hi, lo, :, hidden : 2 * hidden] = (hidden_grad * silu).astype(BF16)
        ag[g, hi, lo, :, 2 * hidden :] = (silu * pre_up).astype(BF16)
        send(ag.at[g, hi, lo], ag.at[g, hi, lo], g_s.at[j, 0], g_r.at[j, 0], dp_far)

    def spread_out(j):
        g = group[j]
        arrived(ag.at[g, 1 - hi, lo], g_r.at[j, 0], g_s.at[j, 0], dp_far)
        send(ag.at[g, :, lo], ag.at[g, :, lo], g_s.at[j, 1], g_r.at[j, 1], dp_near)

    def back(j):
        g = group[j]
        arrived(ag.at[g, :, 1 - lo], g_r.at[j, 1], g_s.at[j, 1], dp_near)
        h = ag[g].reshape(rows, 3 * hidden)
        slot = 8 if j == 3 else g
        for t, (a, b) in enumerate(((2 * hidden, 3 * hidden), (0, 2 * hidden))):
            yp[g, t] = dot(h[:, a:b], wf[:, a:b], 1, 1).astype(BF16).reshape(4, CAP, chunk)
            if j >= 3:
                send(yp.at[g, t], rs.at[slot, t], di_s.at[j, t], d_r.at[slot, t], inward, is_edge)

    def cross():
        send(act.at[low], act_in.at[low], sh_s.at[0], sh_r.at[0], sec_next, sx == 3)
        send(cot.at[low], cot_in.at[low], sh_s.at[2], sh_r.at[2], sec_prev, sx == 0)

        @pl.when(is_via)
        def _():
            arrived(via_in, sh_r.at[6], sh_s.at[6], sec_skip)

        for k in range(VIA):
            at = pl.ds(k * piece, piece)
            send(via_in.at[at], via_out.at[at], v_s.at[2, k], v_r.at[2, k], sec_over, is_via)

    def pass_on(k):
        at = pl.ds(k * piece, piece)

        @pl.when(is_via)
        def _():
            arrived(via_out.at[at], v_r.at[2, k], v_s.at[2, k], sec_over)

        send(via_out.at[at], act_in.at[parts[k]], v_s.at[3, k], v_r.at[0, k], sec_prev, sx == 1)
        send(via_out.at[at], cot_in.at[parts[k]], v_s.at[3, k], v_r.at[1, k], sec_next, sx == 2)

    def add(g, t, slot):
        yp[g, t] = (yp[g, t].astype(F32) + rs[slot, t].astype(F32)).astype(BF16)

    def chain(j, pred, s, dev, slot=None):
        g = group[j]
        slot = g if slot is None else slot
        for t in range(2):

            @pl.when(pred)
            def _():
                arrived(rs.at[g, t], d_r.at[g, t], do_s.at[0, t], inward)
                add(g, t, g)

            send(yp.at[g, t], rs.at[slot, t], s.at[j, t], d_r.at[slot, t], dev, pred)

    def home(src, e, k, pred=None):
        for r in range(3):
            there = lax.rem(d + r + 1, 4)
            send(src.at[:, there], fin.at[e, :, :, own_at], e_s.at[k, r], e_r.at[k, r], dp_dev[r], pred)

        def own():
            fin[e, :, :, own_at] = src[:, d]

        if pred is None:
            own()
        else:
            pl.when(pred)(own)

    def finish(pred, both):
        @pl.when(pred)
        def _():
            for t in range(2):
                arrived(rs.at[z, t], d_r.at[z, t], do_s.at[0, t], inward)
                add(z, t, z)
                if both:
                    arrived(rs.at[8, t], d_r.at[8, t], do_s.at[0, t], outward)
                    add(z, t, 8)

        home(yp.at[z], half, 0, pred)

    for j in range(8):
        receive(j, 0)
        receive(j, 1)
        front(j)
        if j >= 1:
            pair(j - 1)
        if j >= 2:
            middle(j - 2)
        if j >= 3:
            spread_out(j - 3)
        if j >= 4:
            back(j - 4)
    pair(7)
    middle(6)
    spread_out(5)
    back(4)
    middle(7)
    spread_out(6)
    back(5)
    spread_out(7)
    chain(1, is_inner, di_s, inward)
    finish(is_inner, True)
    back(6)
    chain(3, is_inner, di_s, inward)
    chain(2, is_inner, do_s, outward)
    back(7)
    chain(6, is_inner, di_s, inward)
    cross()
    chain(4, is_inner, do_s, outward)
    finish(is_edge, False)
    chain(1, is_edge, do_s, beyond, 9)
    chain(7, is_inner, di_s, inward)
    chain(5, is_inner, do_s, outward)
    chain(2, is_edge, do_s, outward, 9)

    pass_on(0)
    pass_on(1)
    h_all = ag[...].reshape(8 * rows, 3 * hidden)
    x_all = xg[:, :, 0].reshape(8 * rows, chunk)
    dw_mine[:, : 2 * hidden] = dot(x_all, h_all[:, : 2 * hidden], 0, 0)
    g_all = xg[:, :, 1].reshape(8 * rows, chunk)
    dw_mine[:, 2 * hidden :] = dot(g_all, h_all[:, 2 * hidden :], 0, 0)
    for k in range(3):
        at = pl.ds(pl.multiple_of(hidden * k + (1 - c) * cols, cols), cols)
        dw_send[k] = dw_mine[:, at].astype(BF16)
        send(dw_send.at[k], dw_in.at[k], q_s.at[k], q_r.at[k], sibling)

    def leave(e, k):
        for r in range(3):
            there = lax.rem(d + 3 - r, 4)
            at = pl.ds(pl.multiple_of(there * chunk, 128), chunk)
            arrived(fin.at[e, :, :, at], e_r.at[k, r], e_s.at[k, r], dp_dev[r])
        at = pl.ds(pl.multiple_of(e * CAP, CAP), CAP)
        pick_half = e == 0
        gate = jnp.where(pick_half, slot_gates[:CAP], slot_gates[CAP:])
        root = jnp.where(pick_half, inv_root[:CAP], inv_root[CAP:])
        ysend[at] = (gate * fin[e, 0].astype(F32)).astype(BF16)
        send(ysend.at[at], yin.at[at], x_s.at[0, k], x_r.at[0, k], sec_next)
        d_rows = fin[e, 1].astype(F32)
        n_rows = normed[at]
        spread = jnp.mean(n_rows * d_rows, axis=1, keepdims=True)
        dsend[at] = (root * (d_rows - n_rows * spread)).astype(BF16)
        send(dsend.at[at], din.at[at], x_s.at[1, k], x_r.at[1, k], sec_prev)

    for k in range(2, VIA):
        pass_on(k)
    leave(half, 0)

    for t in range(2):
        arrived(rs.at[9, t], d_r.at[9, t], do_s.at[0, t], outward)
    home(rs.at[9], 1 - half, 1)
    leave(1 - half, 1)

    for k, out in enumerate((d_gate_out, d_up_out, d_down_out)):
        arrived(dw_in.at[k], q_r.at[k], q_s.at[k], sibling)
        at = pl.ds(pl.multiple_of(hidden * k + c * cols, cols), cols)
        out[...] = (dw_mine[:, at] + dw_in[k].astype(F32)).astype(BF16)

    for t, (out, kept, pick, extra, dev) in enumerate(
        ((next_act, act_in, pick_prev, yin, sec_next), (prev_grad, cot_in, pick_next, din, sec_prev))
    ):
        arrived(pick, sh_r.at[4 + t], sh_s.at[4 + t], dev)
        arrived(kept.at[low], sh_r.at[2 * t], sh_s.at[2 * t], dev)
        for k, part in enumerate(parts):
            arrived(kept.at[part], v_r.at[t, k], v_s.at[t, k], dev)
        for k, e in ((0, half), (1, 1 - half)):
            at = pl.ds(pl.multiple_of(e * CAP, CAP), CAP)
            arrived(extra.at[at], x_r.at[t, k], x_s.at[t, k], dev)
        out[...] = (kept[...].astype(F32) + dot(pick[...], extra[...], 0, 0)).astype(BF16)

    for pred, build in pending:
        if pred is None:
            build().wait_send()
        else:
            pl.when(pred)(lambda build=build: build().wait_send())


def per_device(act, cotangent, expert_ids, gate_values, w_gate, w_up, w_down_t):
    tokens, width = act.shape[1:]
    depth, cols = w_gate.shape[1:]
    chunk, hidden = width // 4, 2 * cols
    vmem = pl.BlockSpec(memory_space=pltpu.VMEM)
    anywhere = pl.BlockSpec(memory_space=pltpu.HBM)
    dma = pltpu.SemaphoreType.DMA
    slots = EXPERTS * CAP
    topk = expert_ids.shape[2]
    outs = pl.pallas_call(
        kernel,
        name="moe_relay",
        out_shape=[
            jax.ShapeDtypeStruct((tokens, width), BF16),
            jax.ShapeDtypeStruct((tokens, width), BF16),
            jax.ShapeDtypeStruct((depth, cols), BF16),
            jax.ShapeDtypeStruct((depth, cols), BF16),
            jax.ShapeDtypeStruct((depth, cols), BF16),
        ],
        in_specs=[anywhere] * 7,
        out_specs=[vmem] * 5,
        scratch_shapes=[
            pltpu.VMEM((tokens, width), BF16),
            pltpu.VMEM((tokens, width), BF16),
            pltpu.VMEM((topk, tokens), jnp.int32),
            pltpu.VMEM((topk, tokens), F32),
            pltpu.VMEM((depth, 3 * hidden), BF16),
            pltpu.VMEM((EXPERTS, 2, CAP, width), BF16),
            pltpu.VMEM((EXPERTS, 2, 2, 2, CAP, chunk), BF16),
            pltpu.VMEM((8, 2, 2, 2, CAP, chunk), BF16),
            pltpu.VMEM((slots, tokens), BF16),
            pltpu.VMEM((slots, tokens), BF16),
            pltpu.VMEM((slots, tokens), BF16),
            pltpu.VMEM((tokens, width), BF16),
            pltpu.VMEM((tokens, width), BF16),
            pltpu.VMEM((VIA * CAP, width), BF16),
            pltpu.VMEM((VIA * CAP, width), BF16),
            pltpu.VMEM((slots, width), F32),
            pltpu.VMEM((8, 2, CAP, 3 * hidden), BF16),
            pltpu.VMEM((8, 2, 2, CAP, 3 * hidden), F32),
            pltpu.VMEM((8, 2, CAP, 3 * hidden), BF16),
            pltpu.VMEM((8, CAP, 3 * hidden), BF16),
            pltpu.VMEM((8, CAP, 3 * hidden), BF16),
            pltpu.VMEM((8, 2, 2, CAP, 3 * hidden), BF16),
            pltpu.VMEM((8, 2, 4, CAP, chunk), BF16),
            pltpu.VMEM((10, 2, 4, CAP, chunk), BF16),
            pltpu.VMEM((EXPERTS, 2, CAP, width), BF16),
            pltpu.VMEM((slots, width), BF16),
            pltpu.VMEM((slots, width), BF16),
            pltpu.VMEM((slots, width), BF16),
            pltpu.VMEM((slots, width), BF16),
            pltpu.VMEM((depth, 3 * hidden), F32),
            pltpu.VMEM((3, depth, cols), BF16),
            pltpu.VMEM((3, depth, cols), BF16),
            dma((7,)),
            dma((3,)), dma((3,)),
            dma((3,)), dma((3,)),
            dma((7,)), dma((7,)),
            dma((4, VIA)), dma((3, VIA)),
            dma((8, 2)), dma((9, 2)), dma((8, 2)),
            dma((8, 2)), dma((8, 2)),
            dma((8, 2)), dma((8, 2)),
            dma((8, 2)), dma((8, 2)), dma((10, 2)),
            dma((2, 3)), dma((2, 3)),
            dma((2, 2)), dma((2, 2)),
            dma((3,)), dma((3,)),
        ],
        compiler_params=pltpu.CompilerParams(
            collective_id=0, has_side_effects=True, vmem_limit_bytes=62 * 2**20
        ),
    )(
        act[0],
        cotangent[0],
        jnp.swapaxes(expert_ids[0], 0, 1),
        jnp.swapaxes(gate_values[0], 0, 1),
        w_gate[0],
        w_up[0],
        w_down_t[0],
    )
    return tuple(out[None] for out in outs)


def solution(mesh):
    rows = P("section", ("expert", "dp"), None)
    weights = P("section", "dp", "expert")
    return jax.shard_map(
        per_device,
        mesh=mesh,
        in_specs=(rows,) * 4 + (weights,) * 3,
        out_specs=(rows,) * 2 + (weights,) * 3,
        check_vma=False,
    )
```
